128 devices in a mesh: row: 4 (over y_hi, core), col: 8 (over y_lo, z), depth: 4 (over x).
Axes of the slice: x: 4, y: 4 (y_hi: 2, y_lo: 2; y = y_hi * 2 + y_lo), z: 4, core: 2. Of those that a mesh axis runs over, the one named last changes fastest.
Arguments:
- out_factor: bfloat16 [8192, 8192], P('row', ('depth', 'col')), may hold values from -1 to 4
- gradient: bfloat16 [8192, 8192], P(('depth', 'row'), 'col'), may hold values from -6 to 6
- in_factor: bfloat16 [8192, 8192], P('col', ('row', 'depth')), may hold values from -1 to 4
Outputs:
- update: float32 [8192, 8192], P(('row', 'depth'), 'col')
The draws below stay inside these ranges and needn't reach their ends.
All inputs are finite; a program needn't handle non-finite values.
Results may differ from the reference program's by a relative error of at most 0.0029.
Values may be sent and summed in bfloat16 or wider, within the bound.
A program may use at most 128 MiB of HBM per device.

```python
import math
import jax
import jax.numpy as jnp
from jax import lax

D = 8192
ROWS = 8192


def inverse_factor(noise, strength, rows, cols):
    row_index = lax.broadcasted_iota(jnp.int32, (rows, cols), 0)
    col_index = lax.broadcasted_iota(jnp.int32, (rows, cols), 1)
    diagonal = jnp.where(row_index == col_index, strength, 0.0)
    return diagonal + noise * (0.5 / math.sqrt(cols))


def draw_out_factor(key, part):
    key = jax.random.fold_in(key, 11)
    first, second = jax.random.split(key)
    noise = jax.random.normal(first, (ROWS, D), jnp.float32)
    strength = jnp.exp(jax.random.uniform(second, (ROWS, 1), jnp.float32, math.log(0.5), math.log(2.0)))
    return inverse_factor(noise, strength, ROWS, D).astype(jnp.bfloat16)


def draw_in_factor(key, part):
    key = jax.random.fold_in(key, 23)
    first, second = jax.random.split(key)
    noise = jax.random.normal(first, (D, D), jnp.float32)
    strength = jnp.exp(jax.random.uniform(second, (D, 1), jnp.float32, math.log(0.5), math.log(2.0)))
    return inverse_factor(noise, strength, D, D).astype(jnp.bfloat16)


def steps_of(stream_key, dims, cuts, smallest, top_value):
    def one(position, parts):
        heights = jax.random.uniform(jax.random.fold_in(jax.random.fold_in(stream_key, 6), position), (parts,), jnp.float32, smallest / len(cuts), top_value / len(cuts))
        return jnp.repeat(jnp.exp(heights), dims[position] // parts).reshape((-1,) + (1,) * (len(dims) - position - 1))

    level = one(*cuts[0])
    for cut in cuts[1:]:
        level = level * one(*cut)
    return level


def bell_draw(key, dims, scale, reach, cuts=(), kind=jnp.bfloat16):
    level = steps_of(key, dims, cuts, -0.22, 0.18) if cuts else 1.0
    array = jax.random.normal(key, dims, jnp.float32) * scale * level
    return jnp.minimum(jnp.maximum(array, -reach), reach).astype(kind)


def setup_inputs(seed: int = 0) -> dict:
    splits = jax.random.split(jax.random.key(seed), 4)
    return {
        "out_factor": draw_out_factor(jax.random.fold_in(splits[3], 71), 0),
        "gradient": bell_draw(splits[1], (D, D), 1.0, 6.0, ((0, 16), (1, 8))),
        "in_factor": draw_in_factor(jax.random.fold_in(splits[3], 71), 0),
    }


def reference(out_factor, gradient, in_factor):
    hidden = jnp.dot(out_factor, gradient, preferred_element_type=jnp.float32).astype(jnp.bfloat16)
    return jnp.dot(hidden, in_factor, preferred_element_type=jnp.float32)
```

```python
import jax
import jax.numpy as jnp
from jax import lax
from jax.sharding import PartitionSpec as P


def shards(out_factor, gradient, in_factor):
    rows, cols = lax.axis_size("row"), lax.axis_size("col")
    pair = cols // rows
    factor_block = lax.all_gather(out_factor, "col", axis=1, tiled=True)
    grad_block = lax.all_gather(gradient, "row", axis=0, tiled=True)
    terms = jnp.dot(factor_block, grad_block, preferred_element_type=jnp.float32)
    hidden = lax.psum_scatter(terms, "depth", scatter_dimension=0, tiled=True).astype(jnp.bfloat16)
    hidden_rows = lax.all_gather(hidden, "row", axis=0, tiled=True)
    in_block = lax.all_gather(in_factor, "depth", axis=1, tiled=True)
    partial_terms = jnp.dot(hidden_rows, in_block, preferred_element_type=jnp.float32)
    height, width = hidden.shape
    chunks = partial_terms.reshape(rows, height, pair, width).transpose(0, 2, 1, 3).reshape(cols * height, width)
    summed = lax.psum_scatter(chunks, "col", scatter_dimension=0, tiled=True)
    moves = [
        (row * cols + to_row * pair + part, to_row * cols + row * pair + part)
        for row in range(rows)
        for to_row in range(rows)
        for part in range(pair)
    ]
    return lax.ppermute(summed, ("row", "col"), moves)


def solution(mesh):
    in_specs = (P("row", ("depth", "col")), P(("depth", "row"), "col"), P("col", ("row", "depth")))
    out_specs = P(("row", "depth"), "col")
    return jax.shard_map(shards, mesh=mesh, in_specs=in_specs, out_specs=out_specs, check_vma=False)
```

```python
import functools
import jax
import jax.numpy as jnp
from jax import lax
from jax.experimental import pallas as pl
from jax.experimental.pallas import tpu as pltpu
from jax.sharding import PartitionSpec as P

MESH = pl.DeviceIdType.MESH
BF16 = jnp.bfloat16
F32 = jnp.float32
PARTS = 2
TILE = 256


def place(x, y, z, core):
    return ((y // 2) * 2 + core, (y % 2) * 4 + z, x)


def kernel(a_in, g_in, b_in, out, a_all, g_all, b_all, terms, terms_in, own_h, h_all, u_out, u_in,
           swap_s, swap_r, az_s, az_r, ac_s, ac_r, g_s, g_r, turn_s, turn_r, bx_s, bx_r, bc_s, bc_r,
           t_s, t_r, h_s, h_r, u_s, u_r):
    row, col, x = lax.axis_index("row"), lax.axis_index("col"), lax.axis_index("depth")
    y_hi, core, y_lo, z = row // 2, row % 2, col // 4, col % 4
    y = y_hi * 2 + y_lo
    other = 1 - core
    sibling = place(x, y, z, other)
    straight = core == y_lo
    height = own_h.shape[0]
    part = height // PARTS

    def remote(src, dst, send, recv, to):
        return pltpu.make_async_remote_copy(
            src_ref=src, dst_ref=dst, send_sem=send, recv_sem=recv, device_id=to, device_id_type=MESH
        )

    barrier = pltpu.get_barrier_semaphore()
    partners = [sibling]
    for step in range(1, 4):
        partners.append(place(x, (y + step) % 4, z, 0))
        partners.append(place(x, (y + step) % 4, z, 1))
        partners.append(place(x, y, (z + step) % 4, core))
        partners.append(place((x + step) % 4, y, z, core))
        partners.append(place(x, (y + 2) % 4, (z + step) % 4, core))
    for partner in partners:
        pl.semaphore_signal(barrier, inc=1, device_id=partner, device_id_type=MESH)
    pl.semaphore_wait(barrier, len(partners))

    def span(index):
        return pl.ds(index * part, part)

    mine_a = core * 4 + z
    swapped = place(x, y_hi * 2 + core, z, y_lo)

    def swap(p):
        src, dst = a_in.at[:, span(p), :], a_all.at[mine_a, :, span(p), :]
        to_slot = a_all.at[y_lo * 4 + z, :, span(p), :]
        return (
            remote(src, to_slot, swap_s.at[p], swap_r.at[p], swapped),
            pltpu.make_async_copy(src, dst, swap_r.at[p]),
        )

    def swap_start(p):
        away, here = swap(p)

        @pl.when(straight)
        def _():
            here.start()

        @pl.when(jnp.logical_not(straight))
        def _():
            away.start()

    def swap_wait(p):
        src, dst = a_in.at[:, span(p), :], a_all.at[mine_a, :, span(p), :]

        @pl.when(straight)
        def _():
            pltpu.make_async_copy(src, dst, swap_r.at[p]).wait()

        @pl.when(jnp.logical_not(straight))
        def _():
            arrived = remote(src, dst, swap_s.at[p], swap_r.at[p], swapped)
            arrived.wait_recv()
            arrived.wait_send()

    def along_z(p, step):
        ref = a_all.at[mine_a, :, span(p), :]
        return remote(ref, ref, az_s.at[p, step - 1], az_r.at[p, step - 1], place(x, y, (z + step) % 4, core))

    def along_z_wait(p, step):
        ref = a_all.at[core * 4 + (z + 4 - step) % 4, :, span(p), :]
        remote(ref, ref, az_s.at[p, step - 1], az_r.at[p, step - 1], sibling).wait_recv()

    def across_a(p, step):
        ref = a_all.at[core * 4 + (z + 4 - step) % 4, :, span(p), :]
        return remote(ref, ref, ac_s.at[p, step], ac_r.at[p, step], sibling)

    def across_a_wait(p, step):
        ref = a_all.at[other * 4 + (z + 4 - step) % 4, :, span(p), :]
        remote(ref, ref, ac_s.at[p, step], ac_r.at[p, step], sibling).wait_recv()

    def spread_start(src, dst, send, recv):
        for step in (2, 1, 3):
            remote(src, dst, send.at[step], recv.at[row], place(x, (y + step) % 4, z, y_lo)).start()

        @pl.when(straight)
        def _():
            pltpu.make_async_copy(src, dst, recv.at[row]).start()

        @pl.when(jnp.logical_not(straight))
        def _():
            remote(src, dst, send.at[0], recv.at[row], sibling).start()

    def spread_sent(src, dst, send, recv):
        for step in (1, 2, 3):
            remote(src, dst, send.at[step], recv.at[row], sibling).wait_send()

        @pl.when(jnp.logical_not(straight))
        def _():
            remote(src, dst, send.at[0], recv.at[row], sibling).wait_send()

    def spread_wait(slots, send, recv):
        for slot in range(4):
            local = jnp.logical_and(straight, row == slot)

            @pl.when(local)
            def _():
                pltpu.make_async_copy(slots(slot), slots(slot), recv.at[slot]).wait()

            @pl.when(jnp.logical_not(local))
            def _():
                remote(slots(slot), slots(slot), send.at[0], recv.at[slot], sibling).wait_recv()

    turned = place(x, core * 2 + y_hi, z, y_lo)
    still = jnp.logical_and(y_hi == y_lo, y_lo == core)

    def turn_start():
        @pl.when(still)
        def _():
            pltpu.make_async_copy(b_in, b_all.at[core, x], turn_r).start()

        @pl.when(jnp.logical_not(still))
        def _():
            remote(b_in, b_all.at[y_lo, x], turn_s, turn_r, turned).start()

    def turn_wait():
        @pl.when(still)
        def _():
            pltpu.make_async_copy(b_in, b_all.at[core, x], turn_r).wait()

        @pl.when(jnp.logical_not(still))
        def _():
            arrived = remote(b_in, b_all.at[core, x], turn_s, turn_r, turned)
            arrived.wait_recv()
            arrived.wait_send()

    def along_x(step):
        ref = b_all.at[core, x]
        return remote(ref, ref, bx_s.at[step - 1], bx_r.at[step - 1], place((x + step) % 4, y, z, core))

    def along_x_wait(step):
        ref = b_all.at[core, (x + 4 - step) % 4]
        remote(ref, ref, bx_s.at[step - 1], bx_r.at[step - 1], sibling).wait_recv()

    def across_b(step):
        ref = b_all.at[core, (x + 4 - step) % 4]
        return remote(ref, ref, bc_s.at[step], bc_r.at[step], sibling)

    def across_b_wait(step):
        ref = b_all.at[other, (x + 4 - step) % 4]
        remote(ref, ref, bc_s.at[step], bc_r.at[step], sibling).wait_recv()

    def give(p, step):
        return remote(
            terms.at[step, span(p), :], terms_in.at[step - 1, span(p), :], t_s.at[p, step - 1], t_r.at[p, step - 1],
            place((x + step) % 4, y, z, core),
        )

    def update_to(p, upper, half):
        return remote(
            u_out.at[upper, half, span(p), :], u_in.at[z, span(p), :], u_s.at[p, upper, half], u_r.at[p, z],
            place(x, upper * 2 + y_lo, y_hi * 2 + half, core),
        )

    def is_own(upper, half):
        return jnp.logical_and(upper == y_hi, y_hi * 2 + half == z)

    for p in range(PARTS):
        swap_start(p)
    spread_start(g_in, g_all.at[row], g_s, g_r)
    turn_start()
    for p in range(PARTS):
        swap_wait(p)
        for step in (2, 1, 3):
            along_z(p, step).start()
        across_a(p, 0).start()
    turn_wait()
    for step in (2, 1, 3):
        along_x(step).start()
    across_b(0).start()

    def first_product(p, step):
        owner = (x + step) % 4

        def tile(index, _):
            columns = pl.ds(pl.multiple_of(index * TILE, TILE), TILE)
            left = jnp.concatenate([a_all[slot, owner, span(p), :] for slot in range(8)], axis=1)
            right = jnp.concatenate([g_all[slot, :, columns] for slot in range(4)], axis=0)
            terms[step, span(p), columns] = jnp.dot(left, right, preferred_element_type=F32)
            return 0

        lax.fori_loop(0, own_h.shape[1] // TILE, tile, 0)

    def second_product(p, upper, half):
        def tile(index, _):
            columns = pl.ds(pl.multiple_of((index % 2) * TILE, TILE), TILE)
            left = jnp.concatenate([h_all[upper * 2 + slot, span(p), :] for slot in range(2)], axis=1)
            right = jnp.concatenate([b_all[slot, half * 2 + index // 2, :, columns] for slot in range(2)], axis=0)
            target = pl.ds(pl.multiple_of(index * TILE, TILE), TILE)
            u_out[upper, half, span(p), target] = jnp.dot(left, right, preferred_element_type=F32).astype(BF16)
            return 0

        lax.fori_loop(0, own_h.shape[1] // TILE, tile, 0)

    for p in range(PARTS):
        for step in (1, 3, 2):
            along_z_wait(p, step)
            across_a(p, step).start()
        if p == 0:
            spread_wait(lambda slot: g_all.at[slot], g_s, g_r)
        for step in range(4):
            across_a_wait(p, step)
        for step in (2, 1, 3):
            first_product(p, step)
            give(p, step).start()
        first_product(p, 0)

    for step in (1, 3, 2):
        along_x_wait(step)
        across_b(step).start()

    for p in range(PARTS):
        for step in (1, 3, 2):
            give(p, step).wait_recv()
        total = terms[0, span(p), :]
        for step in range(3):
            total += terms_in[step, span(p), :]
        own_h[span(p), :] = total.astype(BF16)
        spread_start(own_h.at[span(p), :], h_all.at[row, span(p), :], h_s.at[p], h_r.at[p])

    for step in range(4):
        across_b_wait(step)
    for p in range(PARTS):
        spread_wait(lambda slot: h_all.at[slot, span(p), :], h_s.at[p], h_r.at[p])
        for upper in range(2):
            for half in range(2):
                second_product(p, upper, half)
                own = is_own(upper, half)

                @pl.when(own)
                def _():
                    pltpu.make_async_copy(
                        u_out.at[upper, half, span(p), :], u_in.at[z, span(p), :], u_r.at[p, z]
                    ).start()

                @pl.when(jnp.logical_not(own))
                def _():
                    update_to(p, upper, half).start()

    for p in range(PARTS):
        for source in range(4):
            ref = u_in.at[source, span(p), :]
            local = jnp.logical_and(source == z, y_hi == z // 2)

            @pl.when(local)
            def _():
                pltpu.make_async_copy(ref, ref, u_r.at[p, source]).wait()

            @pl.when(jnp.logical_not(local))
            def _():
                remote(ref, ref, u_s.at[p, 0, 0], u_r.at[p, source], sibling).wait_recv()

        total = u_in[0, span(p), :].astype(F32)
        for source in range(1, 4):
            total += u_in[source, span(p), :].astype(F32)
        out[span(p), :] = total

    spread_sent(g_in, g_all.at[row], g_s, g_r)
    for step in (1, 2, 3):
        along_x(step).wait_send()
    for step in range(4):
        across_b(step).wait_send()
    for p in range(PARTS):
        for step in (1, 2, 3):
            along_z(p, step).wait_send()
            give(p, step).wait_send()
        for step in range(4):
            across_a(p, step).wait_send()
        spread_sent(own_h.at[span(p), :], h_all.at[row, span(p), :], h_s.at[p], h_r.at[p])
        for upper in range(2):
            for half in range(2):
                @pl.when(jnp.logical_not(is_own(upper, half)))
                def _():
                    update_to(p, upper, half).wait_send()


def shards(out_factor, gradient, in_factor):
    height, width = gradient.shape
    dma = pltpu.SemaphoreType.DMA
    return pl.pallas_call(
        kernel,
        out_shape=jax.ShapeDtypeStruct((height, width), F32),
        in_specs=[pl.BlockSpec(memory_space=pl.ANY)] * 3,
        out_specs=pl.BlockSpec(memory_space=pltpu.VMEM),
        scratch_shapes=[
            pltpu.VMEM((8, 4, height, out_factor.shape[1]), BF16),
            pltpu.VMEM((4, height, width), BF16),
            pltpu.VMEM((2, 4) + in_factor.shape, BF16),
            pltpu.VMEM((4, height, width), F32),
            pltpu.VMEM((3, height, width), F32),
            pltpu.VMEM((height, width), BF16),
            pltpu.VMEM((4, height, width), BF16),
            pltpu.VMEM((2, 2, height, width), BF16),
            pltpu.VMEM((4, height, width), BF16),
            dma((PARTS,)), dma((PARTS,)),
            dma((PARTS, 3)), dma((PARTS, 3)),
            dma((PARTS, 4)), dma((PARTS, 4)),
            dma((4,)), dma((4,)),
            dma, dma,
            dma((3,)), dma((3,)),
            dma((4,)), dma((4,)),
            dma((PARTS, 3)), dma((PARTS, 3)),
            dma((PARTS, 4)), dma((PARTS, 4)),
            dma((PARTS, 2, 2)), dma((PARTS, 4)),
        ],
        compiler_params=pltpu.CompilerParams(
            collective_id=0, has_side_effects=True, vmem_limit_bytes=60 * 2**20
        ),
        cost_estimate=pl.CostEstimate(flops=2 * 2**34, bytes_accessed=8 * 2**20, transcendentals=0),
    )(out_factor.reshape(4, height, -1), gradient, in_factor)


def solution(mesh):
    in_specs = (P("row", ("depth", "col")), P(("depth", "row"), "col"), P("col", ("row", "depth")))
    out_specs = P(("row", "depth"), "col")
    return jax.shard_map(shards, mesh=mesh, in_specs=in_specs, out_specs=out_specs, check_vma=False)
```

```python
import functools
import jax
import jax.numpy as jnp
from jax import lax
from jax.experimental import pallas as pl
from jax.experimental.pallas import tpu as pltpu
from jax.sharding import PartitionSpec as P

MESH = pl.DeviceIdType.MESH
BF16 = jnp.bfloat16
F32 = jnp.float32
PARTS = 4
LOADS = 2
SIDES = 2
TILE = 256


def place(x, y, z, core):
    return ((y // 2) * 2 + core, (y % 2) * 4 + z, x)


def kernel(a_in, g_in, b_in, out, a_all, g_all, b_all, terms, terms_in, far, far_in, own_h, h_all, u_out, u_in,
           swap_s, swap_r, az_s, az_r, ac_s, ac_r, g_s, g_r, turn_s, turn_r, bx_s, bx_r, bc_s, bc_r,
           t_s, t_r, h_s, h_r, u_s, u_r):
    row, col, x = lax.axis_index("row"), lax.axis_index("col"), lax.axis_index("depth")
    y_hi, core, y_lo, z = row // 2, row % 2, col // 4, col % 4
    y = y_hi * 2 + y_lo
    other = 1 - core
    sibling = place(x, y, z, other)
    straight = core == y_lo
    height = own_h.shape[0]
    part = height // PARTS
    load = height // LOADS
    side = own_h.shape[1] // SIDES
    quarter = b_in.shape[1]

    def remote(src, dst, send, recv, to):
        return pltpu.make_async_remote_copy(
            src_ref=src, dst_ref=dst, send_sem=send, recv_sem=recv, device_id=to, device_id_type=MESH
        )

    barrier = pltpu.get_barrier_semaphore()
    partners = [sibling]
    for step in range(1, 4):
        partners.append(place(x, (y + step) % 4, z, 0))
        partners.append(place(x, (y + step) % 4, z, 1))
        partners.append(place(x, y, (z + step) % 4, core))
        partners.append(place((x + step) % 4, y, z, core))
        partners.append(place(x, (y + 2) % 4, (z + step) % 4, core))
    for partner in partners:
        pl.semaphore_signal(barrier, inc=1, device_id=partner, device_id_type=MESH)
    pl.semaphore_wait(barrier, len(partners))

    def span(index):
        return pl.ds(index * part, part)

    def rows_of(index):
        return pl.ds(index * load, load)

    def half_of(index):
        return pl.ds(index * side, side)

    mine_a = core * 4 + z
    swapped = place(x, y_hi * 2 + core, z, y_lo)

    def swap(p):
        src, dst = a_in.at[:, rows_of(p), :], a_all.at[mine_a, :, rows_of(p), :]
        to_slot = a_all.at[y_lo * 4 + z, :, rows_of(p), :]
        return (
            remote(src, to_slot, swap_s.at[p], swap_r.at[p], swapped),
            pltpu.make_async_copy(src, dst, swap_r.at[p]),
        )

    def swap_start(p):
        away, here = swap(p)

        @pl.when(straight)
        def _():
            here.start()

        @pl.when(jnp.logical_not(straight))
        def _():
            away.start()

    def swap_wait(p):
        src, dst = a_in.at[:, rows_of(p), :], a_all.at[mine_a, :, rows_of(p), :]

        @pl.when(straight)
        def _():
            pltpu.make_async_copy(src, dst, swap_r.at[p]).wait()

        @pl.when(jnp.logical_not(straight))
        def _():
            arrived = remote(src, dst, swap_s.at[p], swap_r.at[p], swapped)
            arrived.wait_recv()
            arrived.wait_send()

    def along_z(p, step):
        ref = a_all.at[mine_a, :, rows_of(p), :]
        return remote(ref, ref, az_s.at[p, step - 1], az_r.at[p, step - 1], place(x, y, (z + step) % 4, core))

    def along_z_wait(p, step):
        ref = a_all.at[core * 4 + (z + 4 - step) % 4, :, rows_of(p), :]
        remote(ref, ref, az_s.at[p, step - 1], az_r.at[p, step - 1], sibling).wait_recv()

    def across_a(p, step):
        ref = a_all.at[core * 4 + (z + 4 - step) % 4, :, rows_of(p), :]
        return remote(ref, ref, ac_s.at[p, step], ac_r.at[p, step], sibling)

    def across_a_wait(p, step):
        ref = a_all.at[other * 4 + (z + 4 - step) % 4, :, rows_of(p), :]
        remote(ref, ref, ac_s.at[p, step], ac_r.at[p, step], sibling).wait_recv()

    def spread_start(src, dst, send, recv):
        for step in (2, 1, 3):
            remote(src, dst, send.at[step], recv.at[row], place(x, (y + step) % 4, z, y_lo)).start()

        @pl.when(straight)
        def _():
            pltpu.make_async_copy(src, dst, recv.at[row]).start()

        @pl.when(jnp.logical_not(straight))
        def _():
            remote(src, dst, send.at[0], recv.at[row], sibling).start()

    def spread_sent(src, dst, send, recv):
        for step in (1, 2, 3):
            remote(src, dst, send.at[step], recv.at[row], sibling).wait_send()

        @pl.when(jnp.logical_not(straight))
        def _():
            remote(src, dst, send.at[0], recv.at[row], sibling).wait_send()

    def spread_wait(slots, send, recv):
        for slot in range(4):
            local = jnp.logical_and(straight, row == slot)

            @pl.when(local)
            def _():
                pltpu.make_async_copy(slots(slot), slots(slot), recv.at[slot]).wait()

            @pl.when(jnp.logical_not(local))
            def _():
                remote(slots(slot), slots(slot), send.at[0], recv.at[slot], sibling).wait_recv()

    odd = x % 2
    turned = place(x, ((core + odd) % 2) * 2 + y_hi, z, y_lo)
    still = jnp.logical_and(jnp.logical_and(y_hi == y_lo, y_lo == core), odd == 0)

    def turn_start():
        @pl.when(still)
        def _():
            pltpu.make_async_copy(b_in, b_all.at[core, x], turn_r).start()

        @pl.when(jnp.logical_not(still))
        def _():
            remote(b_in, b_all.at[y_lo, x], turn_s, turn_r, turned).start()

    def turn_wait():
        @pl.when(still)
        def _():
            pltpu.make_async_copy(b_in, b_all.at[core, x], turn_r).wait()

        @pl.when(jnp.logical_not(still))
        def _():
            arrived = remote(b_in, b_all.at[core, x], turn_s, turn_r, turned)
            arrived.wait_recv()
            arrived.wait_send()

    def along_x(step):
        ref = b_all.at[core, x]
        return remote(ref, ref, bx_s.at[step - 1], bx_r.at[step - 1], place((x + step) % 4, y, z, core))

    def along_x_wait(step):
        ref = b_all.at[core, (x + 4 - step) % 4]
        remote(ref, ref, bx_s.at[step - 1], bx_r.at[step - 1], sibling).wait_recv()

    def across_b(step):
        ref = b_all.at[core, (x + 4 - step) % 4]
        return remote(ref, ref, bc_s.at[step], bc_r.at[step], sibling)

    def across_b_wait(step):
        ref = b_all.at[other, (x + 4 - step) % 4]
        remote(ref, ref, bc_s.at[step], bc_r.at[step], sibling).wait_recv()

    def give(p, j, step):
        block = (span(p), half_of(j))
        if step == 2:
            src, dst = far.at[block], far_in.at[block]
        else:
            src, dst = terms.at[(step // 2 + 1,) + block], terms_in.at[(step // 2,) + block]
        return remote(src, dst, t_s.at[p, j, step - 1], t_r.at[p, j, step - 1], place((x + step) % 4, y, z, core))

    def owner_z(block):
        return ((y_hi + block) % 2) * 2 + block // 2

    def update_refs(p, upper, block):
        return (
            u_out.at[upper, span(p), pl.ds(block * quarter, quarter)],
            u_in.at[z, span(p), pl.ds((block % 2) * quarter, quarter)],
        )

    def update_to(p, upper, block):
        src, dst = update_refs(p, upper, block)
        return remote(
            src, dst, u_s.at[p, upper, block], u_r.at[p, z, block % 2],
            place(x, upper * 2 + y_lo, owner_z(block), core),
        )

    def is_own(upper, block):
        return jnp.logical_and(upper == y_hi, owner_z(block) == z)

    for p in range(LOADS):
        swap_start(p)
    turn_start()
    for p in range(LOADS):
        swap_wait(p)
        for step in (2, 1, 3):
            along_z(p, step).start()
        across_a(p, 0).start()
    turn_wait()
    for step in (2, 1, 3):
        along_x(step).start()
    across_b(0).start()
    for j in range(SIDES):
        spread_start(g_in.at[:, half_of(j)], g_all.at[row, :, half_of(j)], g_s.at[j], g_r.at[j])

    def first_product(p, j, step):
        owner = (x + step) % 4

        def tile(index, _):
            columns = pl.ds(pl.multiple_of(j * side + index * TILE, TILE), TILE)
            left = jnp.concatenate([a_all[slot, owner, span(p), :] for slot in range(8)], axis=1)
            right = jnp.concatenate([g_all[slot, :, columns] for slot in range(4)], axis=0)
            product = jnp.dot(left, right, preferred_element_type=F32)
            if step == 2:
                far[span(p), columns] = product.astype(BF16)
            else:
                terms[(step + 1) // 2, span(p), columns] = product
            return 0

        lax.fori_loop(0, side // TILE, tile, 0)

    def second_product(p, upper, block):
        def tile(index, _):
            columns = pl.ds(pl.multiple_of(index * TILE, TILE), TILE)
            left = jnp.concatenate([h_all[upper * 2 + slot, span(p), :] for slot in range(2)], axis=1)
            right = jnp.concatenate([b_all[slot, block, :, columns] for slot in range(2)], axis=0)
            target = pl.ds(pl.multiple_of(block * quarter + index * TILE, TILE), TILE)
            u_out[upper, span(p), target] = jnp.dot(left, right, preferred_element_type=F32).astype(BF16)
            return 0

        lax.fori_loop(0, quarter // TILE, tile, 0)

    def arrive_a(p):
        for step in (1, 3, 2):
            along_z_wait(p, step)
            across_a(p, step).start()
        for step in range(4):
            across_a_wait(p, step)

    def arrive_g(j):
        spread_wait(lambda slot: g_all.at[slot, :, half_of(j)], g_s.at[j], g_r.at[j])

    def send_terms(p, j):
        for step in (2, 1, 3):
            first_product(p, j, step)
            give(p, j, step).start()
        first_product(p, j, 0)

    arrive_a(0)
    arrive_g(0)
    for p in range(PARTS // 2):
        send_terms(p, 0)
    for step in (1, 3, 2):
        along_x_wait(step)
        across_b(step).start()
    arrive_a(1)
    arrive_g(1)
    for p in range(PARTS // 2):
        send_terms(p, 1)
    for p in range(PARTS // 2, PARTS):
        for j in range(SIDES):
            send_terms(p, j)

    for p in range(PARTS):
        for j in range(SIDES):
            for step in (1, 3, 2):
                give(p, j, step).wait_recv()
        total = terms[0, span(p), :] + far_in[span(p), :].astype(F32)
        for step in range(2):
            total += terms_in[step, span(p), :]
        own_h[span(p), :] = total.astype(BF16)
        spread_start(own_h.at[span(p), :], h_all.at[row, span(p), :], h_s.at[p], h_r.at[p])

    for step in range(4):
        across_b_wait(step)
    for p in range(PARTS):
        spread_wait(lambda slot: h_all.at[slot, span(p), :], h_s.at[p], h_r.at[p])
        for upper in range(2):
            for block in range(4):
                second_product(p, upper, block)
                own = is_own(upper, block)

                @pl.when(own)
                def _():
                    src, dst = update_refs(p, upper, block)
                    pltpu.make_async_copy(src, dst, u_r.at[p, z, block % 2]).start()

                @pl.when(jnp.logical_not(own))
                def _():
                    update_to(p, upper, block).start()

    for p in range(PARTS):
        for source in range(4):
            for half in range(2):
                ref = u_in.at[source, span(p), pl.ds(half * quarter, quarter)]
                local = jnp.logical_and(source == z, (z // 2 + half) % 2 == y_hi)

                @pl.when(local)
                def _():
                    pltpu.make_async_copy(ref, ref, u_r.at[p, source, half]).wait()

                @pl.when(jnp.logical_not(local))
                def _():
                    remote(ref, ref, u_s.at[p, 0, 0], u_r.at[p, source, half], sibling).wait_recv()

        total = u_in[0, span(p), :].astype(F32)
        for source in range(1, 4):
            total += u_in[source, span(p), :].astype(F32)
        out[span(p), :] = total

    for j in range(SIDES):
        spread_sent(g_in.at[:, half_of(j)], g_all.at[row, :, half_of(j)], g_s.at[j], g_r.at[j])
    for step in (1, 2, 3):
        along_x(step).wait_send()
    for step in range(4):
        across_b(step).wait_send()
    for p in range(LOADS):
        for step in (1, 2, 3):
            along_z(p, step).wait_send()
        for step in range(4):
            across_a(p, step).wait_send()
    for p in range(PARTS):
        for j in range(SIDES):
            for step in (1, 2, 3):
                give(p, j, step).wait_send()
        spread_sent(own_h.at[span(p), :], h_all.at[row, span(p), :], h_s.at[p], h_r.at[p])
        for upper in range(2):
            for block in range(4):
                @pl.when(jnp.logical_not(is_own(upper, block)))
                def _():
                    update_to(p, upper, block).wait_send()


def shards(out_factor, gradient, in_factor):
    height, width = gradient.shape
    dma = pltpu.SemaphoreType.DMA
    return pl.pallas_call(
        kernel,
        out_shape=jax.ShapeDtypeStruct((height, width), F32),
        in_specs=[pl.BlockSpec(memory_space=pl.ANY)] * 3,
        out_specs=pl.BlockSpec(memory_space=pltpu.VMEM),
        scratch_shapes=[
            pltpu.VMEM((8, 4, height, out_factor.shape[1]), BF16),
            pltpu.VMEM((4, height, width), BF16),
            pltpu.VMEM((2, 4) + in_factor.shape, BF16),
            pltpu.VMEM((3, height, width), F32),
            pltpu.VMEM((2, height, width), F32),
            pltpu.VMEM((height, width), BF16),
            pltpu.VMEM((height, width), BF16),
            pltpu.VMEM((height, width), BF16),
            pltpu.VMEM((4, height, width), BF16),
            pltpu.VMEM((2, height, 2 * width), BF16),
            pltpu.VMEM((4, height, width), BF16),
            dma((LOADS,)), dma((LOADS,)),
            dma((LOADS, 3)), dma((LOADS, 3)),
            dma((LOADS, 4)), dma((LOADS, 4)),
            dma((SIDES, 4)), dma((SIDES, 4)),
            dma, dma,
            dma((3,)), dma((3,)),
            dma((4,)), dma((4,)),
            dma((PARTS, SIDES, 3)), dma((PARTS, SIDES, 3)),
            dma((PARTS, 4)), dma((PARTS, 4)),
            dma((PARTS, 2, 4)), dma((PARTS, 4, 2)),
        ],
        compiler_params=pltpu.CompilerParams(
            collective_id=0, has_side_effects=True, vmem_limit_bytes=60 * 2**20
        ),
        cost_estimate=pl.CostEstimate(flops=2 * 2**34, bytes_accessed=8 * 2**20, transcendentals=0),
    )(out_factor.reshape(4, height, -1), gradient, in_factor)


def solution(mesh):
    in_specs = (P("row", ("depth", "col")), P(("depth", "row"), "col"), P("col", ("row", "depth")))
    out_specs = P(("row", "depth"), "col")
    return jax.shard_map(shards, mesh=mesh, in_specs=in_specs, out_specs=out_specs, check_vma=False)
```

```python
import functools
import jax
import jax.numpy as jnp
from jax import lax
from jax.experimental import pallas as pl
from jax.experimental.pallas import tpu as pltpu
from jax.sharding import PartitionSpec as P

MESH = pl.DeviceIdType.MESH
BF16 = jnp.bfloat16
F32 = jnp.float32
PARTS = 4
LOADS = 2
SIDES = 2
TILE = 512


def place(x, y, z, core):
    return ((y // 2) * 2 + core, (y % 2) * 4 + z, x)


def kernel(a_in, g_in, b_in, out, a_all, g_all, b_all, terms, terms_in, far, far_in, own_h, h_all, u_out, u_own, u_in, cross_out, cross_in,
           swap_s, swap_r, az_s, az_r, ac_s, ac_r, g_s, g_r, turn_s, turn_r, bx_s, bx_r, bc_s, bc_r,
           t_s, t_r, h_s, h_r, u_s, u_r, c_s, c_r):
    row, col, x = lax.axis_index("row"), lax.axis_index("col"), lax.axis_index("depth")
    y_hi, core, y_lo, z = row // 2, row % 2, col // 4, col % 4
    y = y_hi * 2 + y_lo
    other = 1 - core
    sibling = place(x, y, z, other)
    straight = core == y_lo
    height = own_h.shape[0]
    part = height // PARTS
    load = height // LOADS
    side = own_h.shape[1] // SIDES
    quarter = b_in.shape[1]

    def remote(src, dst, send, recv, to):
        return pltpu.make_async_remote_copy(
            src_ref=src, dst_ref=dst, send_sem=send, recv_sem=recv, device_id=to, device_id_type=MESH
        )

    barrier = pltpu.get_barrier_semaphore()
    partners = [sibling]
    for step in range(1, 4):
        partners.append(place(x, (y + step) % 4, z, 0))
        partners.append(place(x, (y + step) % 4, z, 1))
        partners.append(place(x, y, (z + step) % 4, core))
        partners.append(place((x + step) % 4, y, z, core))
    for partner in partners:
        pl.semaphore_signal(barrier, inc=1, device_id=partner, device_id_type=MESH)
    pl.semaphore_wait(barrier, len(partners))

    def span(index):
        return pl.ds(index * part, part)

    def rows_of(index):
        return pl.ds(index * load, load)

    def half_of(index):
        return pl.ds(index * side, side)

    mine_a = core * 4 + z
    swapped = place(x, y_hi * 2 + core, z, y_lo)

    def swap(p):
        src, dst = a_in.at[:, rows_of(p), :], a_all.at[mine_a, :, rows_of(p), :]
        to_slot = a_all.at[y_lo * 4 + z, :, rows_of(p), :]
        return (
            remote(src, to_slot, swap_s.at[p], swap_r.at[p], swapped),
            pltpu.make_async_copy(src, dst, swap_r.at[p]),
        )

    def swap_start(p):
        away, here = swap(p)

        @pl.when(straight)
        def _():
            here.start()

        @pl.when(jnp.logical_not(straight))
        def _():
            away.start()

    def swap_wait(p):
        src, dst = a_in.at[:, rows_of(p), :], a_all.at[mine_a, :, rows_of(p), :]

        @pl.when(straight)
        def _():
            pltpu.make_async_copy(src, dst, swap_r.at[p]).wait()

        @pl.when(jnp.logical_not(straight))
        def _():
            arrived = remote(src, dst, swap_s.at[p], swap_r.at[p], swapped)
            arrived.wait_recv()
            arrived.wait_send()

    def along_z(p, step):
        ref = a_all.at[mine_a, :, rows_of(p), :]
        return remote(ref, ref, az_s.at[p, step - 1], az_r.at[p, step - 1], place(x, y, (z + step) % 4, core))

    def along_z_wait(p, step):
        ref = a_all.at[core * 4 + (z + 4 - step) % 4, :, rows_of(p), :]
        remote(ref, ref, az_s.at[p, step - 1], az_r.at[p, step - 1], sibling).wait_recv()

    def across_a(p, step):
        ref = a_all.at[core * 4 + (z + 4 - step) % 4, :, rows_of(p), :]
        return remote(ref, ref, ac_s.at[p, step], ac_r.at[p, step], sibling)

    def across_a_wait(p, step):
        ref = a_all.at[other * 4 + (z + 4 - step) % 4, :, rows_of(p), :]
        remote(ref, ref, ac_s.at[p, step], ac_r.at[p, step], sibling).wait_recv()

    def spread_start(src, dst, send, recv):
        for step in (2, 1, 3):
            remote(src, dst, send.at[step], recv.at[row], place(x, (y + step) % 4, z, y_lo)).start()

        @pl.when(straight)
        def _():
            pltpu.make_async_copy(src, dst, recv.at[row]).start()

        @pl.when(jnp.logical_not(straight))
        def _():
            remote(src, dst, send.at[0], recv.at[row], sibling).start()

    def spread_sent(src, dst, send, recv):
        for step in (1, 2, 3):
            remote(src, dst, send.at[step], recv.at[row], sibling).wait_send()

        @pl.when(jnp.logical_not(straight))
        def _():
            remote(src, dst, send.at[0], recv.at[row], sibling).wait_send()

    def spread_wait(slots, send, recv):
        for slot in range(4):
            local = jnp.logical_and(straight, row == slot)

            @pl.when(local)
            def _():
                pltpu.make_async_copy(slots(slot), slots(slot), recv.at[slot]).wait()

            @pl.when(jnp.logical_not(local))
            def _():
                remote(slots(slot), slots(slot), send.at[0], recv.at[slot], sibling).wait_recv()

    odd = x % 2
    turned = place(x, ((core + odd) % 2) * 2 + y_hi, z, y_lo)
    still = jnp.logical_and(jnp.logical_and(y_hi == y_lo, y_lo == core), odd == 0)

    def b_rows(index):
        return pl.ds(index * (b_in.shape[0] // 2), b_in.shape[0] // 2)

    def turn_start(bit):
        src, dst = b_in.at[b_rows(bit), :], b_all.at[core, x, b_rows(bit), :]

        @pl.when(still)
        def _():
            pltpu.make_async_copy(src, dst, turn_r.at[bit]).start()

        @pl.when(jnp.logical_not(still))
        def _():
            to_slot = b_all.at[y_lo, x, b_rows(bit), :]
            remote(src, to_slot, turn_s.at[bit], turn_r.at[bit], turned).start()

    def turn_wait(bit):
        src, dst = b_in.at[b_rows(bit), :], b_all.at[core, x, b_rows(bit), :]

        @pl.when(still)
        def _():
            pltpu.make_async_copy(src, dst, turn_r.at[bit]).wait()

        @pl.when(jnp.logical_not(still))
        def _():
            arrived = remote(src, dst, turn_s.at[bit], turn_r.at[bit], turned)
            arrived.wait_recv()
            arrived.wait_send()

    def along_x(step, part):
        ref = b_all.at[core, x, b_rows(part), :]
        return remote(ref, ref, bx_s.at[step // 2, part], bx_r.at[step // 2, part], place((x + step) % 4, y, z, core))

    def along_x_wait(step, part):
        ref = b_all.at[core, (x + 4 - step) % 4, b_rows(part), :]
        remote(ref, ref, bx_s.at[step // 2, part], bx_r.at[step // 2, part], sibling).wait_recv()

    def pass_x(step, part):
        ref = b_all.at[core, (x + 4 - step) % 4, b_rows(part), :]
        return remote(ref, ref, bx_s.at[2, part], bx_r.at[2, part], place((x + step) % 4, y, z, core))

    def pass_x_wait(part):
        ref = b_all.at[core, (x + 2) % 4, b_rows(part), :]
        remote(ref, ref, bx_s.at[2, part], bx_r.at[2, part], sibling).wait_recv()

    def across_b(step):
        ref = b_all.at[core, (x + 4 - step) % 4]
        return remote(ref, ref, bc_s.at[step], bc_r.at[step], sibling)

    def across_b_wait(step):
        ref = b_all.at[other, (x + 4 - step) % 4]
        remote(ref, ref, bc_s.at[step], bc_r.at[step], sibling).wait_recv()

    def give(p, j, step):
        block = (span(p), half_of(j))
        if step == 2:
            src, dst, to = far.at[block], far_in.at[block], relay(j)
        else:
            src, dst, to = terms.at[(step // 2 + 1,) + block], terms_in.at[(step // 2,) + block], step
        return remote(src, dst, t_s.at[p, j, step - 1], t_r.at[p, j, step - 1], place((x + to) % 4, y, z, core))

    def relay(j):
        return 1 if j == 0 else 3

    def block_of(owner):
        return (owner % 2) * 2 + (owner // 2 + y_hi) % 2

    def update_to(p, away, step):
        return remote(
            u_out.at[step - 1, away, span(p), :], u_in.at[step - 1, away, span(p), :],
            u_s.at[p, away, step - 1], u_r.at[p, away, step - 1], place(x, y, (z + step) % 4, core),
        )

    def cross(p):
        return remote(
            cross_out.at[span(p), :], cross_in.at[span(p), :], c_s.at[p], c_r.at[p], place(x, (y + 2) % 4, z, core)
        )

    for p in range(LOADS):
        turn_start(p)
        swap_start(p)
    for p in range(LOADS):
        turn_wait(p)
        for step in (1, 3):
            along_x(step, p).start()
        swap_wait(p)
        for step in (2, 1, 3):
            along_z(p, step).start()
        across_a(p, 0).start()
    across_b(0).start()
    for j in range(SIDES):
        spread_start(g_in.at[:, half_of(j)], g_all.at[row, :, half_of(j)], g_s.at[j], g_r.at[j])

    def first_product(p, j, step):
        owner = (x + step) % 4

        def tile(index, _):
            columns = pl.ds(pl.multiple_of(j * side + index * TILE, TILE), TILE)
            left = jnp.concatenate([a_all[slot, owner, span(p), :] for slot in range(8)], axis=1)
            right = jnp.concatenate([g_all[slot, :, columns] for slot in range(4)], axis=0)
            product = jnp.dot(left, right, preferred_element_type=F32)
            if step == 2:
                far[span(p), columns] = product.astype(BF16)
            elif step == relay(j):
                terms[(step + 1) // 2, span(p), columns] = product + far_in[span(p), columns].astype(F32)
            else:
                terms[(step + 1) // 2, span(p), columns] = product
            return 0

        lax.fori_loop(0, side // TILE, tile, 0)

    def second_product(p, away, step):
        upper = (y_hi + away) % 2
        block = block_of((z + step) % 4)
        left = jnp.concatenate([h_all[upper * 2 + slot, span(p), :] for slot in range(2)], axis=1)
        right = jnp.concatenate([b_all[slot, block] for slot in range(2)], axis=0)
        product = jnp.dot(left, right, preferred_element_type=F32)
        if step == 0:
            u_own[away, span(p), :] = product
        else:
            u_out[step - 1, away, span(p), :] = product.astype(BF16)

    def share_b():
        for step, bit in ((1, 1), (3, 0)):
            along_x_wait(step, bit)
            across_b(step).start()
        for bit in range(2):
            pass_x_wait(bit)
        across_b(2).start()

    def arrive_a(p):
        for step in (1, 3, 2):
            along_z_wait(p, step)
            across_a(p, step).start()
        for step in range(4):
            across_a_wait(p, step)

    def arrive_g(j):
        spread_wait(lambda slot: g_all.at[slot, :, half_of(j)], g_s.at[j], g_r.at[j])

    def send_far(p, j):
        first_product(p, j, 2)
        give(p, j, 2).start()

    def send_near(p, j):
        for step in (4 - relay(j), relay(j)):
            if step == relay(j):
                give(p, j, 2).wait_recv()
            first_product(p, j, step)
            give(p, j, step).start()
        first_product(p, j, 0)

    def send_terms(chunks):
        send_far(*chunks[0])
        for now, later in zip(chunks, chunks[1:] + [None]):
            if later is not None:
                send_far(*later)
            send_near(*now)

    def sum_terms(p):
        for j in range(SIDES):
            for step in (1, 3):
                give(p, j, step).wait_recv()
        total = terms[0, span(p), :]
        for step in range(2):
            total += terms_in[step, span(p), :]
        own_h[span(p), :] = total.astype(BF16)
        spread_start(own_h.at[span(p), :], h_all.at[row, span(p), :], h_s.at[p], h_r.at[p])

    arrive_a(0)
    for step, bit in ((1, 0), (3, 1)):
        along_x_wait(step, bit)
        pass_x(step, bit).start()
    arrive_g(0)
    early = list(range(PARTS // 2))
    send_terms([(p, 0) for p in early])
    arrive_a(1)
    arrive_g(1)
    def send_update(p):
        spread_wait(lambda slot: h_all.at[slot, span(p), :], h_s.at[p], h_r.at[p])
        for away in (1, 0):
            for step in (2, 1, 3):
                second_product(p, away, step)
                update_to(p, away, step).start()
            second_product(p, away, 0)

    def sum_update(p, away):
        for step in (1, 3, 2):
            update_to(p, away, step).wait_recv()
        total = u_own[away, span(p), :]
        for step in range(3):
            total += u_in[step, away, span(p), :].astype(F32)
        return total

    half = (z // 2 + y_hi) % 2

    def place_update(p):
        cross_out[span(p), :] = sum_update(p, 1)
        cross(p).start()
        out[span(p), pl.ds(pl.multiple_of(half * quarter, quarter), quarter)] = sum_update(p, 0)

    send_far(0, 1)
    send_far(1, 1)
    send_near(0, 1)
    send_far(2, 0)
    send_near(1, 1)
    share_b()
    send_far(2, 1)
    send_near(2, 0)
    sum_terms(0)
    send_far(3, 0)
    send_near(2, 1)
    sum_terms(1)
    send_far(3, 1)
    send_near(3, 0)
    send_near(3, 1)
    sum_terms(2)
    for step in range(4):
        across_b_wait(step)
    for p in range(PARTS):
        send_update(p)
        if p == 0:
            sum_terms(3)
        if p >= 1:
            place_update(p - 1)
    place_update(PARTS - 1)
    for p in range(PARTS):
        cross(p).wait_recv()
        out[span(p), pl.ds(pl.multiple_of((1 - half) * quarter, quarter), quarter)] = cross_in[span(p), :]

    for j in range(SIDES):
        spread_sent(g_in.at[:, half_of(j)], g_all.at[row, :, half_of(j)], g_s.at[j], g_r.at[j])
    for step in (1, 3):
        for bit in range(2):
            along_x(step, bit).wait_send()
        pass_x(step, step // 2).wait_send()
    for step in range(4):
        across_b(step).wait_send()
    for p in range(LOADS):
        for step in (1, 2, 3):
            along_z(p, step).wait_send()
        for step in range(4):
            across_a(p, step).wait_send()
    for p in range(PARTS):
        for j in range(SIDES):
            for step in (1, 2, 3):
                give(p, j, step).wait_send()
        spread_sent(own_h.at[span(p), :], h_all.at[row, span(p), :], h_s.at[p], h_r.at[p])
        for away in range(2):
            for step in (1, 2, 3):
                update_to(p, away, step).wait_send()
        cross(p).wait_send()


def shards(out_factor, gradient, in_factor):
    height, width = gradient.shape
    dma = pltpu.SemaphoreType.DMA
    return pl.pallas_call(
        kernel,
        out_shape=jax.ShapeDtypeStruct((height, width), F32),
        in_specs=[pl.BlockSpec(memory_space=pl.ANY)] * 3,
        out_specs=pl.BlockSpec(memory_space=pltpu.VMEM),
        scratch_shapes=[
            pltpu.VMEM((8, 4, height, out_factor.shape[1]), BF16),
            pltpu.VMEM((4, height, width), BF16),
            pltpu.VMEM((2, 4) + in_factor.shape, BF16),
            pltpu.VMEM((3, height, width), F32),
            pltpu.VMEM((2, height, width), F32),
            pltpu.VMEM((height, width), BF16),
            pltpu.VMEM((height, width), BF16),
            pltpu.VMEM((height, width), BF16),
            pltpu.VMEM((4, height, width), BF16),
            pltpu.VMEM((3, 2, height, in_factor.shape[1]), BF16),
            pltpu.VMEM((2, height, in_factor.shape[1]), F32),
            pltpu.VMEM((3, 2, height, in_factor.shape[1]), BF16),
            pltpu.VMEM((height, in_factor.shape[1]), F32),
            pltpu.VMEM((height, in_factor.shape[1]), F32),
            dma((LOADS,)), dma((LOADS,)),
            dma((LOADS, 3)), dma((LOADS, 3)),
            dma((LOADS, 4)), dma((LOADS, 4)),
            dma((SIDES, 4)), dma((SIDES, 4)),
            dma((2,)), dma((2,)),
            dma((3, 2)), dma((3, 2)),
            dma((4,)), dma((4,)),
            dma((PARTS, SIDES, 3)), dma((PARTS, SIDES, 3)),
            dma((PARTS, 4)), dma((PARTS, 4)),
            dma((PARTS, 2, 3)), dma((PARTS, 2, 3)),
            dma((PARTS,)), dma((PARTS,)),
        ],
        compiler_params=pltpu.CompilerParams(
            collective_id=0, has_side_effects=True, vmem_limit_bytes=60 * 2**20
        ),
        cost_estimate=pl.CostEstimate(flops=2 * 2**34, bytes_accessed=8 * 2**20, transcendentals=0),
    )(out_factor.reshape(4, height, -1), gradient, in_factor)


def solution(mesh):
    in_specs = (P("row", ("depth", "col")), P(("depth", "row"), "col"), P("col", ("row", "depth")))
    out_specs = P(("row", "depth"), "col")
    return jax.shard_map(shards, mesh=mesh, in_specs=in_specs, out_specs=out_specs, check_vma=False)
```

```python
import functools
import jax
import jax.numpy as jnp
from jax import lax
from jax.experimental import pallas as pl
from jax.experimental.pallas import tpu as pltpu
from jax.sharding import PartitionSpec as P

MESH = pl.DeviceIdType.MESH
BF16 = jnp.bfloat16
F32 = jnp.float32
PARTS = 4
LOADS = 2
SIDES = 2
TILE = 512


def place(x, y, z, core):
    return ((y // 2) * 2 + core, (y % 2) * 4 + z, x)


def kernel(a_in, g_in, b_in, out, a_all, g_all, b_all, terms, terms_in, far, far_in, own_h, h_all, u_out, u_own, u_in, cross_out, cross_in,
           swap_s, swap_r, az_s, az_r, ac_s, ac_r, g_s, g_r, f_s, turn_s, turn_r, bx_s, bx_r, bc_s, bc_r,
           t_s, t_r, h_s, h_r, u_s, u_r, c_s, c_r):
    row, col, x = lax.axis_index("row"), lax.axis_index("col"), lax.axis_index("depth")
    y_hi, core, y_lo, z = row // 2, row % 2, col // 4, col % 4
    y = y_hi * 2 + y_lo
    other = 1 - core
    sibling = place(x, y, z, other)
    straight = core == y_lo
    height = own_h.shape[0]
    part = height // PARTS
    load = height // LOADS
    side = own_h.shape[1] // SIDES
    quarter = b_in.shape[1]

    def remote(src, dst, send, recv, to):
        return pltpu.make_async_remote_copy(
            src_ref=src, dst_ref=dst, send_sem=send, recv_sem=recv, device_id=to, device_id_type=MESH
        )

    barrier = pltpu.get_barrier_semaphore()
    partners = [sibling]
    for step in range(1, 4):
        partners.append(place(x, (y + step) % 4, z, 0))
        partners.append(place(x, (y + step) % 4, z, 1))
        partners.append(place(x, y, (z + step) % 4, core))
        partners.append(place((x + step) % 4, y, z, core))
    for partner in partners:
        pl.semaphore_signal(barrier, inc=1, device_id=partner, device_id_type=MESH)
    pl.semaphore_wait(barrier, len(partners))

    def span(index):
        return pl.ds(index * part, part)

    def rows_of(index):
        return pl.ds(index * load, load)

    def half_of(index):
        return pl.ds(index * side, side)

    mine_a = core * 4 + z
    swapped = place(x, y_hi * 2 + core, z, y_lo)

    def swap(p):
        src, dst = a_in.at[:, rows_of(p), :], a_all.at[mine_a, :, rows_of(p), :]
        to_slot = a_all.at[y_lo * 4 + z, :, rows_of(p), :]
        return (
            remote(src, to_slot, swap_s.at[p], swap_r.at[p], swapped),
            pltpu.make_async_copy(src, dst, swap_r.at[p]),
        )

    def swap_start(p):
        away, here = swap(p)

        @pl.when(straight)
        def _():
            here.start()

        @pl.when(jnp.logical_not(straight))
        def _():
            away.start()

    def swap_wait(p):
        src, dst = a_in.at[:, rows_of(p), :], a_all.at[mine_a, :, rows_of(p), :]

        @pl.when(straight)
        def _():
            pltpu.make_async_copy(src, dst, swap_r.at[p]).wait()

        @pl.when(jnp.logical_not(straight))
        def _():
            arrived = remote(src, dst, swap_s.at[p], swap_r.at[p], swapped)
            arrived.wait_recv()
            arrived.wait_send()

    def along_z(p, step):
        ref = a_all.at[mine_a, :, rows_of(p), :]
        return remote(ref, ref, az_s.at[p, step - 1], az_r.at[p, step - 1], place(x, y, (z + step) % 4, core))

    def along_z_wait(p, step):
        ref = a_all.at[core * 4 + (z + 4 - step) % 4, :, rows_of(p), :]
        remote(ref, ref, az_s.at[p, step - 1], az_r.at[p, step - 1], sibling).wait_recv()

    def across_a(p, step):
        ref = a_all.at[core * 4 + (z + 4 - step) % 4, :, rows_of(p), :]
        return remote(ref, ref, ac_s.at[p, step], ac_r.at[p, step], sibling)

    def across_a_wait(p, step):
        ref = a_all.at[other * 4 + (z + 4 - step) % 4, :, rows_of(p), :]
        remote(ref, ref, ac_s.at[p, step], ac_r.at[p, step], sibling).wait_recv()

    def spread_start(src, dst, send, recv):
        for step in (2, 1, 3):
            remote(src, dst, send.at[step], recv.at[row], place(x, (y + step) % 4, z, y_lo)).start()

        @pl.when(straight)
        def _():
            pltpu.make_async_copy(src, dst, recv.at[row]).start()

        @pl.when(jnp.logical_not(straight))
        def _():
            remote(src, dst, send.at[0], recv.at[row], sibling).start()

    def spread_sent(src, dst, send, recv):
        for step in (1, 2, 3):
            remote(src, dst, send.at[step], recv.at[row], sibling).wait_send()

        @pl.when(jnp.logical_not(straight))
        def _():
            remote(src, dst, send.at[0], recv.at[row], sibling).wait_send()

    def spread_wait(slots, send, recv):
        for slot in range(4):
            local = jnp.logical_and(straight, row == slot)

            @pl.when(local)
            def _():
                pltpu.make_async_copy(slots(slot), slots(slot), recv.at[slot]).wait()

            @pl.when(jnp.logical_not(local))
            def _():
                remote(slots(slot), slots(slot), send.at[0], recv.at[slot], sibling).wait_recv()

    def g_block(slot, j, bit):
        tall = g_in.shape[0] // 2
        return g_all.at[slot, pl.ds(bit * tall, tall), half_of(j)]

    def g_copy(j, bit, step):
        tall = g_in.shape[0] // 2
        to = sibling if step == 0 else place(x, (y + step) % 4, z, y_lo)
        return remote(
            g_in.at[pl.ds(bit * tall, tall), half_of(j)], g_block(row, j, bit),
            g_s.at[j, bit, step // 2 + (step > 0)], g_r.at[j, row, bit], to,
        )

    def g_start(j):
        for step, bit in ((1, 0), (3, 1), (1, 1), (3, 0)):
            g_copy(j, bit, step).start()
        for bit in range(2):
            @pl.when(straight)
            def _():
                src = g_in.at[pl.ds(bit * (g_in.shape[0] // 2), g_in.shape[0] // 2), half_of(j)]
                pltpu.make_async_copy(src, g_block(row, j, bit), g_r.at[j, row, bit]).start()

            @pl.when(jnp.logical_not(straight))
            def _():
                g_copy(j, bit, 0).start()

    def g_sent(j):
        for bit in range(2):
            for step in (1, 3):
                g_copy(j, bit, step).wait_send()

            @pl.when(jnp.logical_not(straight))
            def _():
                g_copy(j, bit, 0).wait_send()

    def g_slot(step, which):
        return ((y + step) % 4) // 2 * 2 + which

    def g_pass(j, which, step):
        ref = g_block(g_slot(4 - step, which), j, step // 2)
        return remote(
            ref, ref, f_s.at[j, which, step // 2], g_r.at[j, g_slot(4 - step, which), step // 2],
            place(x, (y + step) % 4, z, core),
        )

    def g_got(slot, j, bit):
        ref = g_block(slot, j, bit)
        remote(ref, ref, g_s.at[j, bit, 0], g_r.at[j, slot, bit], sibling).wait_recv()

    def g_relay(j):
        @pl.when(jnp.logical_not(straight))
        def _():
            for step in (1, 3):
                for which in range(2):
                    g_got(g_slot(4 - step, which), j, step // 2)
                    g_pass(j, which, step).start()

    def g_relayed(j):
        @pl.when(jnp.logical_not(straight))
        def _():
            for step in (1, 3):
                for which in range(2):
                    g_pass(j, which, step).wait_send()

    def arrive_g(j):
        @pl.when(straight)
        def _():
            for bit in range(2):
                own = g_block(row, j, bit)
                pltpu.make_async_copy(own, own, g_r.at[j, row, bit]).wait()
                g_got(g_slot(0, other), j, bit)
                for which in range(2):
                    g_got(g_slot(2, which), j, bit)

        @pl.when(jnp.logical_not(straight))
        def _():
            for step in (1, 3):
                for which in range(2):
                    g_got(g_slot(4 - step, which), j, 1 - step // 2)

    odd = x % 2
    turned = place(x, ((core + odd) % 2) * 2 + y_hi, z, y_lo)
    still = jnp.logical_and(jnp.logical_and(y_hi == y_lo, y_lo == core), odd == 0)

    def b_rows(index):
        return pl.ds(index * (b_in.shape[0] // 2), b_in.shape[0] // 2)

    def turn_start(bit):
        src, dst = b_in.at[b_rows(bit), :], b_all.at[core, x, b_rows(bit), :]

        @pl.when(still)
        def _():
            pltpu.make_async_copy(src, dst, turn_r.at[bit]).start()

        @pl.when(jnp.logical_not(still))
        def _():
            to_slot = b_all.at[y_lo, x, b_rows(bit), :]
            remote(src, to_slot, turn_s.at[bit], turn_r.at[bit], turned).start()

    def turn_wait(bit):
        src, dst = b_in.at[b_rows(bit), :], b_all.at[core, x, b_rows(bit), :]

        @pl.when(still)
        def _():
            pltpu.make_async_copy(src, dst, turn_r.at[bit]).wait()

        @pl.when(jnp.logical_not(still))
        def _():
            arrived = remote(src, dst, turn_s.at[bit], turn_r.at[bit], turned)
            arrived.wait_recv()
            arrived.wait_send()

    def along_x(step, part):
        ref = b_all.at[core, x, b_rows(part), :]
        return remote(ref, ref, bx_s.at[step // 2, part], bx_r.at[step // 2, part], place((x + step) % 4, y, z, core))

    def along_x_wait(step, part):
        ref = b_all.at[core, (x + 4 - step) % 4, b_rows(part), :]
        remote(ref, ref, bx_s.at[step // 2, part], bx_r.at[step // 2, part], sibling).wait_recv()

    def pass_x(step, part):
        ref = b_all.at[core, (x + 4 - step) % 4, b_rows(part), :]
        return remote(ref, ref, bx_s.at[2, part], bx_r.at[2, part], place((x + step) % 4, y, z, core))

    def pass_x_wait(part):
        ref = b_all.at[core, (x + 2) % 4, b_rows(part), :]
        remote(ref, ref, bx_s.at[2, part], bx_r.at[2, part], sibling).wait_recv()

    def across_b(step):
        ref = b_all.at[core, (x + 4 - step) % 4]
        return remote(ref, ref, bc_s.at[step], bc_r.at[step], sibling)

    def across_b_wait(step):
        ref = b_all.at[other, (x + 4 - step) % 4]
        remote(ref, ref, bc_s.at[step], bc_r.at[step], sibling).wait_recv()

    def give(p, j, step):
        block = (span(p), half_of(j))
        if step == 2:
            src, dst, to = far.at[block], far_in.at[block], relay(j)
        else:
            src, dst, to = terms.at[(step // 2 + 1,) + block], terms_in.at[(step // 2,) + block], step
        return remote(src, dst, t_s.at[p, j, step - 1], t_r.at[p, j, step - 1], place((x + to) % 4, y, z, core))

    def relay(j):
        return 1 if j == 0 else 3

    def block_of(owner):
        return (owner % 2) * 2 + (owner // 2 + y_hi) % 2

    def update_to(p, away, step):
        return remote(
            u_out.at[step - 1, away, span(p), :], u_in.at[step - 1, away, span(p), :],
            u_s.at[p, away, step - 1], u_r.at[p, away, step - 1], place(x, y, (z + step) % 4, core),
        )

    def cross(p):
        return remote(
            cross_out.at[span(p), :], cross_in.at[span(p), :], c_s.at[p], c_r.at[p], place(x, (y + 2) % 4, z, core)
        )

    for p in range(LOADS):
        turn_start(p)
        swap_start(p)
    for p in range(LOADS):
        turn_wait(p)
        for step in (1, 3):
            along_x(step, p).start()
        swap_wait(p)
        for step in (2, 1, 3):
            along_z(p, step).start()
        across_a(p, 0).start()
    across_b(0).start()
    for j in range(SIDES):
        g_start(j)

    def first_product(p, j, step):
        owner = (x + step) % 4

        def tile(index, _):
            columns = pl.ds(pl.multiple_of(j * side + index * TILE, TILE), TILE)
            left = jnp.concatenate([a_all[slot, owner, span(p), :] for slot in range(8)], axis=1)
            right = jnp.concatenate([g_all[slot, :, columns] for slot in range(4)], axis=0)
            product = jnp.dot(left, right, preferred_element_type=F32)
            if step == 2:
                far[span(p), columns] = product.astype(BF16)
            elif step == relay(j):
                terms[(step + 1) // 2, span(p), columns] = product + far_in[span(p), columns].astype(F32)
            else:
                terms[(step + 1) // 2, span(p), columns] = product
            return 0

        lax.fori_loop(0, side // TILE, tile, 0)

    def second_product(p, away, step):
        upper = (y_hi + away) % 2
        block = block_of((z + step) % 4)
        left = jnp.concatenate([h_all[upper * 2 + slot, span(p), :] for slot in range(2)], axis=1)
        right = jnp.concatenate([b_all[slot, block] for slot in range(2)], axis=0)
        product = jnp.dot(left, right, preferred_element_type=F32)
        if step == 0:
            u_own[away, span(p), :] = product
        else:
            u_out[step - 1, away, span(p), :] = product.astype(BF16)

    def share_b():
        for step, bit in ((1, 1), (3, 0)):
            along_x_wait(step, bit)
            across_b(step).start()
        for bit in range(2):
            pass_x_wait(bit)
        across_b(2).start()

    def arrive_a(p):
        for step in (1, 3, 2):
            along_z_wait(p, step)
            across_a(p, step).start()
        for step in range(4):
            across_a_wait(p, step)

    def send_far(p, j):
        first_product(p, j, 2)
        give(p, j, 2).start()

    def send_near(p, j):
        for step in (4 - relay(j), relay(j)):
            if step == relay(j):
                give(p, j, 2).wait_recv()
            first_product(p, j, step)
            give(p, j, step).start()
        first_product(p, j, 0)

    def send_terms(chunks):
        send_far(*chunks[0])
        for now, later in zip(chunks, chunks[1:] + [None]):
            if later is not None:
                send_far(*later)
            send_near(*now)

    def sum_terms(p):
        for j in range(SIDES):
            for step in (1, 3):
                give(p, j, step).wait_recv()
        total = terms[0, span(p), :]
        for step in range(2):
            total += terms_in[step, span(p), :]
        own_h[span(p), :] = total.astype(BF16)
        spread_start(own_h.at[span(p), :], h_all.at[row, span(p), :], h_s.at[p], h_r.at[p])

    g_relay(0)
    arrive_a(0)
    for step, bit in ((1, 0), (3, 1)):
        along_x_wait(step, bit)
        pass_x(step, bit).start()
    g_relay(1)
    arrive_g(0)
    early = list(range(PARTS // 2))
    send_terms([(p, 0) for p in early])
    arrive_a(1)
    arrive_g(1)
    def send_update(p):
        spread_wait(lambda slot: h_all.at[slot, span(p), :], h_s.at[p], h_r.at[p])
        for away in (1, 0):
            for step in (2, 1, 3):
                second_product(p, away, step)
                update_to(p, away, step).start()
            second_product(p, away, 0)

    def sum_update(p, away):
        for step in (1, 3, 2):
            update_to(p, away, step).wait_recv()
        total = u_own[away, span(p), :]
        for step in range(3):
            total += u_in[step, away, span(p), :].astype(F32)
        return total

    half = (z // 2 + y_hi) % 2

    def place_update(p):
        cross_out[span(p), :] = sum_update(p, 1).astype(BF16)
        cross(p).start()
        out[span(p), pl.ds(pl.multiple_of(half * quarter, quarter), quarter)] = sum_update(p, 0)

    send_far(0, 1)
    send_far(1, 1)
    send_near(0, 1)
    send_far(2, 0)
    send_near(1, 1)
    share_b()
    send_far(2, 1)
    send_near(2, 0)
    sum_terms(0)
    send_far(3, 0)
    send_near(2, 1)
    sum_terms(1)
    send_far(3, 1)
    send_near(3, 0)
    send_near(3, 1)
    sum_terms(2)
    for step in range(4):
        across_b_wait(step)
    for p in range(PARTS):
        send_update(p)
        if p == 0:
            sum_terms(3)
        if p >= 1:
            place_update(p - 1)
    place_update(PARTS - 1)
    for p in range(PARTS):
        cross(p).wait_recv()
        out[span(p), pl.ds(pl.multiple_of((1 - half) * quarter, quarter), quarter)] = cross_in[span(p), :].astype(F32)

    for j in range(SIDES):
        g_sent(j)
        g_relayed(j)
    for step in (1, 3):
        for bit in range(2):
            along_x(step, bit).wait_send()
        pass_x(step, step // 2).wait_send()
    for step in range(4):
        across_b(step).wait_send()
    for p in range(LOADS):
        for step in (1, 2, 3):
            along_z(p, step).wait_send()
        for step in range(4):
            across_a(p, step).wait_send()
    for p in range(PARTS):
        for j in range(SIDES):
            for step in (1, 2, 3):
                give(p, j, step).wait_send()
        spread_sent(own_h.at[span(p), :], h_all.at[row, span(p), :], h_s.at[p], h_r.at[p])
        for away in range(2):
            for step in (1, 2, 3):
                update_to(p, away, step).wait_send()
        cross(p).wait_send()


def shards(out_factor, gradient, in_factor):
    height, width = gradient.shape
    dma = pltpu.SemaphoreType.DMA
    return pl.pallas_call(
        kernel,
        out_shape=jax.ShapeDtypeStruct((height, width), F32),
        in_specs=[pl.BlockSpec(memory_space=pl.ANY)] * 3,
        out_specs=pl.BlockSpec(memory_space=pltpu.VMEM),
        scratch_shapes=[
            pltpu.VMEM((8, 4, height, out_factor.shape[1]), BF16),
            pltpu.VMEM((4, height, width), BF16),
            pltpu.VMEM((2, 4) + in_factor.shape, BF16),
            pltpu.VMEM((3, height, width), F32),
            pltpu.VMEM((2, height, width), F32),
            pltpu.VMEM((height, width), BF16),
            pltpu.VMEM((height, width), BF16),
            pltpu.VMEM((height, width), BF16),
            pltpu.VMEM((4, height, width), BF16),
            pltpu.VMEM((3, 2, height, in_factor.shape[1]), BF16),
            pltpu.VMEM((2, height, in_factor.shape[1]), F32),
            pltpu.VMEM((3, 2, height, in_factor.shape[1]), BF16),
            pltpu.VMEM((height, in_factor.shape[1]), BF16),
            pltpu.VMEM((height, in_factor.shape[1]), BF16),
            dma((LOADS,)), dma((LOADS,)),
            dma((LOADS, 3)), dma((LOADS, 3)),
            dma((LOADS, 4)), dma((LOADS, 4)),
            dma((SIDES, 2, 3)), dma((SIDES, 4, 2)), dma((SIDES, 2, 2)),
            dma((2,)), dma((2,)),
            dma((3, 2)), dma((3, 2)),
            dma((4,)), dma((4,)),
            dma((PARTS, SIDES, 3)), dma((PARTS, SIDES, 3)),
            dma((PARTS, 4)), dma((PARTS, 4)),
            dma((PARTS, 2, 3)), dma((PARTS, 2, 3)),
            dma((PARTS,)), dma((PARTS,)),
        ],
        compiler_params=pltpu.CompilerParams(
            collective_id=0, has_side_effects=True, vmem_limit_bytes=60 * 2**20
        ),
        cost_estimate=pl.CostEstimate(flops=2 * 2**34, bytes_accessed=8 * 2**20, transcendentals=0),
    )(out_factor.reshape(4, height, -1), gradient, in_factor)


def solution(mesh):
    in_specs = (P("row", ("depth", "col")), P(("depth", "row"), "col"), P("col", ("row", "depth")))
    out_specs = P(("row", "depth"), "col")
    return jax.shard_map(shards, mesh=mesh, in_specs=in_specs, out_specs=out_specs, check_vma=False)
```

```python
import functools
import jax
import jax.numpy as jnp
from jax import lax
from jax.experimental import pallas as pl
from jax.experimental.pallas import tpu as pltpu
from jax.sharding import PartitionSpec as P

MESH = pl.DeviceIdType.MESH
BF16 = jnp.bfloat16
F32 = jnp.float32
PARTS = 4
LOADS = 2
SIDES = 2
TILE = 512


def place(x, y, z, core):
    return ((y // 2) * 2 + core, (y % 2) * 4 + z, x)


def kernel(a_in, g_in, b_in, out, a_all, g_all, b_all, terms, terms_in, far, far_in, near, near_in, own_h, h_all, u_out, u_own, u_in, cross_out, cross_in,
           swap_s, swap_r, az_s, az_r, ac_s, ac_r, g_s, g_r, f_s, turn_s, turn_r, bx_s, bx_r, bc_s, bc_r,
           t_s, t_r, h_s, h_r, u_s, u_r, c_s, c_r):
    row, col, x = lax.axis_index("row"), lax.axis_index("col"), lax.axis_index("depth")
    y_hi, core, y_lo, z = row // 2, row % 2, col // 4, col % 4
    y = y_hi * 2 + y_lo
    other = 1 - core
    sibling = place(x, y, z, other)
    straight = core == y_lo
    height = own_h.shape[0]
    part = height // PARTS
    load = height // LOADS
    side = own_h.shape[1] // SIDES
    quarter = b_in.shape[1]

    def remote(src, dst, send, recv, to):
        return pltpu.make_async_remote_copy(
            src_ref=src, dst_ref=dst, send_sem=send, recv_sem=recv, device_id=to, device_id_type=MESH
        )

    barrier = pltpu.get_barrier_semaphore()
    partners = [sibling]
    for step in range(1, 4):
        partners.append(place(x, (y + step) % 4, z, 0))
        partners.append(place(x, (y + step) % 4, z, 1))
        partners.append(place(x, y, (z + step) % 4, core))
        partners.append(place((x + step) % 4, y, z, core))
    for partner in partners:
        pl.semaphore_signal(barrier, inc=1, device_id=partner, device_id_type=MESH)
    pl.semaphore_wait(barrier, len(partners))

    def span(index):
        return pl.ds(index * part, part)

    def rows_of(index):
        return pl.ds(index * load, load)

    def half_of(index):
        return pl.ds(index * side, side)

    mine_a = core * 4 + z
    swapped = place(x, y_hi * 2 + core, z, y_lo)

    def swap(p):
        src, dst = a_in.at[:, rows_of(p), :], a_all.at[mine_a, :, rows_of(p), :]
        to_slot = a_all.at[y_lo * 4 + z, :, rows_of(p), :]
        return (
            remote(src, to_slot, swap_s.at[p], swap_r.at[p], swapped),
            pltpu.make_async_copy(src, dst, swap_r.at[p]),
        )

    def swap_start(p):
        away, here = swap(p)

        @pl.when(straight)
        def _():
            here.start()

        @pl.when(jnp.logical_not(straight))
        def _():
            away.start()

    def swap_wait(p):
        src, dst = a_in.at[:, rows_of(p), :], a_all.at[mine_a, :, rows_of(p), :]

        @pl.when(straight)
        def _():
            pltpu.make_async_copy(src, dst, swap_r.at[p]).wait()

        @pl.when(jnp.logical_not(straight))
        def _():
            arrived = remote(src, dst, swap_s.at[p], swap_r.at[p], swapped)
            arrived.wait_recv()
            arrived.wait_send()

    def along_z(p, step):
        ref = a_all.at[mine_a, :, rows_of(p), :]
        return remote(ref, ref, az_s.at[p, step - 1], az_r.at[p, step - 1], place(x, y, (z + step) % 4, core))

    def along_z_wait(p, step):
        ref = a_all.at[core * 4 + (z + 4 - step) % 4, :, rows_of(p), :]
        remote(ref, ref, az_s.at[p, step - 1], az_r.at[p, step - 1], sibling).wait_recv()

    def across_a(p, step):
        ref = a_all.at[core * 4 + (z + 4 - step) % 4, :, rows_of(p), :]
        return remote(ref, ref, ac_s.at[p, step], ac_r.at[p, step], sibling)

    def across_a_wait(p, step):
        ref = a_all.at[other * 4 + (z + 4 - step) % 4, :, rows_of(p), :]
        remote(ref, ref, ac_s.at[p, step], ac_r.at[p, step], sibling).wait_recv()

    def spread_start(src, dst, send, recv):
        for step in (2, 1, 3):
            remote(src, dst, send.at[step], recv.at[row], place(x, (y + step) % 4, z, y_lo)).start()

        @pl.when(straight)
        def _():
            pltpu.make_async_copy(src, dst, recv.at[row]).start()

        @pl.when(jnp.logical_not(straight))
        def _():
            remote(src, dst, send.at[0], recv.at[row], sibling).start()

    def spread_sent(src, dst, send, recv):
        for step in (1, 2, 3):
            remote(src, dst, send.at[step], recv.at[row], sibling).wait_send()

        @pl.when(jnp.logical_not(straight))
        def _():
            remote(src, dst, send.at[0], recv.at[row], sibling).wait_send()

    def spread_wait(slots, send, recv):
        for slot in range(4):
            local = jnp.logical_and(straight, row == slot)

            @pl.when(local)
            def _():
                pltpu.make_async_copy(slots(slot), slots(slot), recv.at[slot]).wait()

            @pl.when(jnp.logical_not(local))
            def _():
                remote(slots(slot), slots(slot), send.at[0], recv.at[slot], sibling).wait_recv()

    def g_block(slot, j, bit):
        tall = g_in.shape[0] // 2
        return g_all.at[slot, pl.ds(bit * tall, tall), half_of(j)]

    def g_copy(j, bit, step):
        tall = g_in.shape[0] // 2
        to = sibling if step == 0 else place(x, (y + step) % 4, z, y_lo)
        return remote(
            g_in.at[pl.ds(bit * tall, tall), half_of(j)], g_block(row, j, bit),
            g_s.at[j, bit, step // 2 + (step > 0)], g_r.at[j, row, bit], to,
        )

    def g_start(j):
        for step, bit in ((1, 0), (3, 1), (1, 1), (3, 0)):
            g_copy(j, bit, step).start()
        for bit in range(2):
            @pl.when(straight)
            def _():
                src = g_in.at[pl.ds(bit * (g_in.shape[0] // 2), g_in.shape[0] // 2), half_of(j)]
                pltpu.make_async_copy(src, g_block(row, j, bit), g_r.at[j, row, bit]).start()

            @pl.when(jnp.logical_not(straight))
            def _():
                g_copy(j, bit, 0).start()

    def g_sent(j):
        for bit in range(2):
            for step in (1, 3):
                g_copy(j, bit, step).wait_send()

            @pl.when(jnp.logical_not(straight))
            def _():
                g_copy(j, bit, 0).wait_send()

    def g_slot(step, which):
        return ((y + step) % 4) // 2 * 2 + which

    def g_pass(j, which, step):
        ref = g_block(g_slot(4 - step, which), j, step // 2)
        return remote(
            ref, ref, f_s.at[j, which, step // 2], g_r.at[j, g_slot(4 - step, which), step // 2],
            place(x, (y + step) % 4, z, core),
        )

    def g_got(slot, j, bit):
        ref = g_block(slot, j, bit)
        remote(ref, ref, g_s.at[j, bit, 0], g_r.at[j, slot, bit], sibling).wait_recv()

    def g_relay(j):
        @pl.when(jnp.logical_not(straight))
        def _():
            for step in (1, 3):
                for which in range(2):
                    g_got(g_slot(4 - step, which), j, step // 2)
                    g_pass(j, which, step).start()

    def g_relayed(j):
        @pl.when(jnp.logical_not(straight))
        def _():
            for step in (1, 3):
                for which in range(2):
                    g_pass(j, which, step).wait_send()

    def arrive_g(j):
        @pl.when(straight)
        def _():
            for bit in range(2):
                own = g_block(row, j, bit)
                pltpu.make_async_copy(own, own, g_r.at[j, row, bit]).wait()
                g_got(g_slot(0, other), j, bit)
                for which in range(2):
                    g_got(g_slot(2, which), j, bit)

        @pl.when(jnp.logical_not(straight))
        def _():
            for step in (1, 3):
                for which in range(2):
                    g_got(g_slot(4 - step, which), j, 1 - step // 2)

    odd = x % 2
    turned = place(x, ((core + odd) % 2) * 2 + y_hi, z, y_lo)
    still = jnp.logical_and(jnp.logical_and(y_hi == y_lo, y_lo == core), odd == 0)

    def b_rows(index):
        return pl.ds(index * (b_in.shape[0] // 2), b_in.shape[0] // 2)

    def turn_start(bit):
        src, dst = b_in.at[b_rows(bit), :], b_all.at[core, x, b_rows(bit), :]

        @pl.when(still)
        def _():
            pltpu.make_async_copy(src, dst, turn_r.at[bit]).start()

        @pl.when(jnp.logical_not(still))
        def _():
            to_slot = b_all.at[y_lo, x, b_rows(bit), :]
            remote(src, to_slot, turn_s.at[bit], turn_r.at[bit], turned).start()

    def turn_wait(bit):
        src, dst = b_in.at[b_rows(bit), :], b_all.at[core, x, b_rows(bit), :]

        @pl.when(still)
        def _():
            pltpu.make_async_copy(src, dst, turn_r.at[bit]).wait()

        @pl.when(jnp.logical_not(still))
        def _():
            arrived = remote(src, dst, turn_s.at[bit], turn_r.at[bit], turned)
            arrived.wait_recv()
            arrived.wait_send()

    def along_x(step, part):
        ref = b_all.at[core, x, b_rows(part), :]
        return remote(ref, ref, bx_s.at[step // 2, part], bx_r.at[step // 2, part], place((x + step) % 4, y, z, core))

    def along_x_wait(step, part):
        ref = b_all.at[core, (x + 4 - step) % 4, b_rows(part), :]
        remote(ref, ref, bx_s.at[step // 2, part], bx_r.at[step // 2, part], sibling).wait_recv()

    def pass_x(step, part):
        ref = b_all.at[core, (x + 4 - step) % 4, b_rows(part), :]
        return remote(ref, ref, bx_s.at[2, part], bx_r.at[2, part], place((x + step) % 4, y, z, core))

    def pass_x_wait(part):
        ref = b_all.at[core, (x + 2) % 4, b_rows(part), :]
        remote(ref, ref, bx_s.at[2, part], bx_r.at[2, part], sibling).wait_recv()

    def across_b(step):
        ref = b_all.at[core, (x + 4 - step) % 4]
        return remote(ref, ref, bc_s.at[step], bc_r.at[step], sibling)

    def across_b_wait(step):
        ref = b_all.at[other, (x + 4 - step) % 4]
        remote(ref, ref, bc_s.at[step], bc_r.at[step], sibling).wait_recv()

    def give(p, j, step):
        block = (span(p), half_of(j))
        if step == 2:
            src, dst, to = far.at[block], far_in.at[block], relay(j)
        elif step != relay(j):
            src, dst, to = near.at[block], near_in.at[block], step
        else:
            src, dst, to = terms.at[(1,) + block], terms_in.at[block], step
        return remote(src, dst, t_s.at[p, j, step - 1], t_r.at[p, j, step - 1], place((x + to) % 4, y, z, core))

    def relay(j):
        return 1 if j == 0 else 3

    def block_of(owner):
        return (owner % 2) * 2 + (owner // 2 + y_hi) % 2

    def update_to(p, away, step):
        return remote(
            u_out.at[step - 1, away, span(p), :], u_in.at[step - 1, away, span(p), :],
            u_s.at[p, away, step - 1], u_r.at[p, away, step - 1], place(x, y, (z + step) % 4, core),
        )

    def cross(p):
        return remote(
            cross_out.at[span(p), :], cross_in.at[span(p), :], c_s.at[p], c_r.at[p], place(x, (y + 2) % 4, z, core)
        )

    for p in range(LOADS):
        turn_start(p)
        swap_start(p)
    for p in range(LOADS):
        turn_wait(p)
        for step in (1, 3):
            along_x(step, p).start()
        swap_wait(p)
        for step in (2, 1, 3):
            along_z(p, step).start()
        across_a(p, 0).start()
    across_b(0).start()
    for j in range(SIDES):
        g_start(j)

    def first_product(p, j, step):
        owner = (x + step) % 4

        def tile(index, _):
            columns = pl.ds(pl.multiple_of(j * side + index * TILE, TILE), TILE)
            left = jnp.concatenate([a_all[slot, owner, span(p), :] for slot in range(8)], axis=1)
            right = jnp.concatenate([g_all[slot, :, columns] for slot in range(4)], axis=0)
            product = jnp.dot(left, right, preferred_element_type=F32)
            if step == 2:
                far[span(p), columns] = product.astype(BF16)
            elif step == relay(j):
                terms[1, span(p), columns] = product + far_in[span(p), columns].astype(F32)
            elif step == 0:
                terms[0, span(p), columns] = product
            else:
                near[span(p), columns] = product.astype(BF16)
            return 0

        lax.fori_loop(0, side // TILE, tile, 0)

    def second_product(p, away, step):
        upper = (y_hi + away) % 2
        block = block_of((z + step) % 4)
        left = jnp.concatenate([h_all[upper * 2 + slot, span(p), :] for slot in range(2)], axis=1)
        right = jnp.concatenate([b_all[slot, block] for slot in range(2)], axis=0)
        product = jnp.dot(left, right, preferred_element_type=F32)
        if step == 0:
            u_own[away, span(p), :] = product
        else:
            u_out[step - 1, away, span(p), :] = product.astype(BF16)

    def share_b():
        for step, bit in ((1, 1), (3, 0)):
            along_x_wait(step, bit)
            across_b(step).start()
        for bit in range(2):
            pass_x_wait(bit)
        across_b(2).start()

    def arrive_a(p):
        for step in (1, 3, 2):
            along_z_wait(p, step)
            across_a(p, step).start()
        for step in range(4):
            across_a_wait(p, step)

    def send_far(p, j):
        first_product(p, j, 2)
        give(p, j, 2).start()

    def send_near(p, j):
        for step in (4 - relay(j), relay(j)):
            if step == relay(j):
                give(p, j, 2).wait_recv()
            first_product(p, j, step)
            give(p, j, step).start()
        first_product(p, j, 0)

    def send_terms(chunks):
        send_far(*chunks[0])
        for now, later in zip(chunks, chunks[1:] + [None]):
            if later is not None:
                send_far(*later)
            send_near(*now)

    def sum_terms(p):
        for j in range(SIDES):
            for step in (1, 3):
                give(p, j, step).wait_recv()
        total = terms[0, span(p), :] + terms_in[span(p), :] + near_in[span(p), :].astype(F32)
        own_h[span(p), :] = total.astype(BF16)
        spread_start(own_h.at[span(p), :], h_all.at[row, span(p), :], h_s.at[p], h_r.at[p])

    g_relay(0)
    arrive_a(0)
    for step, bit in ((1, 0), (3, 1)):
        along_x_wait(step, bit)
        pass_x(step, bit).start()
    g_relay(1)
    arrive_g(0)
    early = list(range(PARTS // 2))
    send_terms([(p, 0) for p in early])
    arrive_a(1)
    arrive_g(1)
    def send_update(p):
        spread_wait(lambda slot: h_all.at[slot, span(p), :], h_s.at[p], h_r.at[p])
        for away in (1, 0):
            for step in (2, 1, 3):
                second_product(p, away, step)
                update_to(p, away, step).start()
            second_product(p, away, 0)

    def sum_update(p, away):
        for step in (1, 3, 2):
            update_to(p, away, step).wait_recv()
        total = u_own[away, span(p), :]
        for step in range(3):
            total += u_in[step, away, span(p), :].astype(F32)
        return total

    half = (z // 2 + y_hi) % 2

    def place_update(p):
        cross_out[span(p), :] = sum_update(p, 1)
        cross(p).start()
        out[span(p), pl.ds(pl.multiple_of(half * quarter, quarter), quarter)] = sum_update(p, 0)

    send_far(0, 1)
    send_far(1, 1)
    send_near(0, 1)
    send_far(2, 0)
    send_near(1, 1)
    share_b()
    send_far(2, 1)
    send_near(2, 0)
    sum_terms(0)
    send_far(3, 0)
    send_near(2, 1)
    sum_terms(1)
    send_far(3, 1)
    send_near(3, 0)
    send_near(3, 1)
    sum_terms(2)
    for step in range(4):
        across_b_wait(step)
    for p in range(PARTS):
        send_update(p)
        if p == 0:
            sum_terms(3)
        if p >= 1:
            place_update(p - 1)
    place_update(PARTS - 1)
    for p in range(PARTS):
        cross(p).wait_recv()
        out[span(p), pl.ds(pl.multiple_of((1 - half) * quarter, quarter), quarter)] = cross_in[span(p), :]

    for j in range(SIDES):
        g_sent(j)
        g_relayed(j)
    for step in (1, 3):
        for bit in range(2):
            along_x(step, bit).wait_send()
        pass_x(step, step // 2).wait_send()
    for step in range(4):
        across_b(step).wait_send()
    for p in range(LOADS):
        for step in (1, 2, 3):
            along_z(p, step).wait_send()
        for step in range(4):
            across_a(p, step).wait_send()
    for p in range(PARTS):
        for j in range(SIDES):
            for step in (1, 2, 3):
                give(p, j, step).wait_send()
        spread_sent(own_h.at[span(p), :], h_all.at[row, span(p), :], h_s.at[p], h_r.at[p])
        for away in range(2):
            for step in (1, 2, 3):
                update_to(p, away, step).wait_send()
        cross(p).wait_send()


def shards(out_factor, gradient, in_factor):
    height, width = gradient.shape
    dma = pltpu.SemaphoreType.DMA
    return pl.pallas_call(
        kernel,
        out_shape=jax.ShapeDtypeStruct((height, width), F32),
        in_specs=[pl.BlockSpec(memory_space=pl.ANY)] * 3,
        out_specs=pl.BlockSpec(memory_space=pltpu.VMEM),
        scratch_shapes=[
            pltpu.VMEM((8, 4, height, out_factor.shape[1]), BF16),
            pltpu.VMEM((4, height, width), BF16),
            pltpu.VMEM((2, 4) + in_factor.shape, BF16),
            pltpu.VMEM((2, height, width), F32),
            pltpu.VMEM((height, width), F32),
            pltpu.VMEM((height, width), BF16),
            pltpu.VMEM((height, width), BF16),
            pltpu.VMEM((height, width), BF16),
            pltpu.VMEM((height, width), BF16),
            pltpu.VMEM((height, width), BF16),
            pltpu.VMEM((4, height, width), BF16),
            pltpu.VMEM((3, 2, height, in_factor.shape[1]), BF16),
            pltpu.VMEM((2, height, in_factor.shape[1]), F32),
            pltpu.VMEM((3, 2, height, in_factor.shape[1]), BF16),
            pltpu.VMEM((height, in_factor.shape[1]), F32),
            pltpu.VMEM((height, in_factor.shape[1]), F32),
            dma((LOADS,)), dma((LOADS,)),
            dma((LOADS, 3)), dma((LOADS, 3)),
            dma((LOADS, 4)), dma((LOADS, 4)),
            dma((SIDES, 2, 3)), dma((SIDES, 4, 2)), dma((SIDES, 2, 2)),
            dma((2,)), dma((2,)),
            dma((3, 2)), dma((3, 2)),
            dma((4,)), dma((4,)),
            dma((PARTS, SIDES, 3)), dma((PARTS, SIDES, 3)),
            dma((PARTS, 4)), dma((PARTS, 4)),
            dma((PARTS, 2, 3)), dma((PARTS, 2, 3)),
            dma((PARTS,)), dma((PARTS,)),
        ],
        compiler_params=pltpu.CompilerParams(
            collective_id=0, has_side_effects=True, vmem_limit_bytes=60 * 2**20
        ),
        cost_estimate=pl.CostEstimate(flops=2 * 2**34, bytes_accessed=8 * 2**20, transcendentals=0),
    )(out_factor.reshape(4, height, -1), gradient, in_factor)


def solution(mesh):
    in_specs = (P("row", ("depth", "col")), P(("depth", "row"), "col"), P("col", ("row", "depth")))
    out_specs = P(("row", "depth"), "col")
    return jax.shard_map(shards, mesh=mesh, in_specs=in_specs, out_specs=out_specs, check_vma=False)
```

```python
import functools
import jax
import jax.numpy as jnp
from jax import lax
from jax.experimental import pallas as pl
from jax.experimental.pallas import tpu as pltpu
from jax.sharding import PartitionSpec as P

MESH = pl.DeviceIdType.MESH
BF16 = jnp.bfloat16
F32 = jnp.float32
PARTS = 4
LOADS = 2
SIDES = 2
TILE = 512


def place(x, y, z, core):
    return ((y // 2) * 2 + core, (y % 2) * 4 + z, x)


def kernel(a_in, g_in, b_in, out, a_all, g_all, b_all, terms, terms_in, far, far_in, own_h, h_all, u_out, u_own, u_in, cross_out, cross_in,
           swap_s, swap_r, az_s, az_r, ac_s, ac_r, g_s, g_r, f_s, turn_s, turn_r, bx_s, bx_r, bc_s, bc_r,
           t_s, t_r, h_s, h_r, u_s, u_r, c_s, c_r):
    row, col, x = lax.axis_index("row"), lax.axis_index("col"), lax.axis_index("depth")
    y_hi, core, y_lo, z = row // 2, row % 2, col // 4, col % 4
    y = y_hi * 2 + y_lo
    other = 1 - core
    sibling = place(x, y, z, other)
    straight = core == y_lo
    height = own_h.shape[0]
    part = height // PARTS
    load = height // LOADS
    side = own_h.shape[1] // SIDES
    quarter = b_in.shape[1]

    def remote(src, dst, send, recv, to):
        return pltpu.make_async_remote_copy(
            src_ref=src, dst_ref=dst, send_sem=send, recv_sem=recv, device_id=to, device_id_type=MESH
        )

    barrier = pltpu.get_barrier_semaphore()
    partners = [sibling]
    for step in range(1, 4):
        partners.append(place(x, (y + step) % 4, z, 0))
        partners.append(place(x, (y + step) % 4, z, 1))
        partners.append(place(x, y, (z + step) % 4, core))
        partners.append(place((x + step) % 4, y, z, core))
    for partner in partners:
        pl.semaphore_signal(barrier, inc=1, device_id=partner, device_id_type=MESH)
    pl.semaphore_wait(barrier, len(partners))

    def span(index):
        return pl.ds(index * part, part)

    def rows_of(index):
        return pl.ds(index * load, load)

    def half_of(index):
        return pl.ds(index * side, side)

    mine_a = core * 4 + z
    swapped = place(x, y_hi * 2 + core, z, y_lo)

    def swap(p):
        src, dst = a_in.at[:, rows_of(p), :], a_all.at[mine_a, :, rows_of(p), :]
        to_slot = a_all.at[y_lo * 4 + z, :, rows_of(p), :]
        return (
            remote(src, to_slot, swap_s.at[p], swap_r.at[p], swapped),
            pltpu.make_async_copy(src, dst, swap_r.at[p]),
        )

    def swap_start(p):
        away, here = swap(p)

        @pl.when(straight)
        def _():
            here.start()

        @pl.when(jnp.logical_not(straight))
        def _():
            away.start()

    def swap_wait(p):
        src, dst = a_in.at[:, rows_of(p), :], a_all.at[mine_a, :, rows_of(p), :]

        @pl.when(straight)
        def _():
            pltpu.make_async_copy(src, dst, swap_r.at[p]).wait()

        @pl.when(jnp.logical_not(straight))
        def _():
            arrived = remote(src, dst, swap_s.at[p], swap_r.at[p], swapped)
            arrived.wait_recv()
            arrived.wait_send()

    def along_z(p, step):
        ref = a_all.at[mine_a, :, rows_of(p), :]
        return remote(ref, ref, az_s.at[p, step - 1], az_r.at[p, step - 1], place(x, y, (z + step) % 4, core))

    def along_z_wait(p, step):
        ref = a_all.at[core * 4 + (z + 4 - step) % 4, :, rows_of(p), :]
        remote(ref, ref, az_s.at[p, step - 1], az_r.at[p, step - 1], sibling).wait_recv()

    def across_a(p, step):
        ref = a_all.at[core * 4 + (z + 4 - step) % 4, :, rows_of(p), :]
        return remote(ref, ref, ac_s.at[p, step], ac_r.at[p, step], sibling)

    def across_a_wait(p, step):
        ref = a_all.at[other * 4 + (z + 4 - step) % 4, :, rows_of(p), :]
        remote(ref, ref, ac_s.at[p, step], ac_r.at[p, step], sibling).wait_recv()

    def spread_start(src, dst, send, recv):
        for step in (2, 1, 3):
            remote(src, dst, send.at[step], recv.at[row], place(x, (y + step) % 4, z, y_lo)).start()

        @pl.when(straight)
        def _():
            pltpu.make_async_copy(src, dst, recv.at[row]).start()

        @pl.when(jnp.logical_not(straight))
        def _():
            remote(src, dst, send.at[0], recv.at[row], sibling).start()

    def spread_sent(src, dst, send, recv):
        for step in (1, 2, 3):
            remote(src, dst, send.at[step], recv.at[row], sibling).wait_send()

        @pl.when(jnp.logical_not(straight))
        def _():
            remote(src, dst, send.at[0], recv.at[row], sibling).wait_send()

    def spread_wait(slots, send, recv):
        for slot in range(4):
            local = jnp.logical_and(straight, row == slot)

            @pl.when(local)
            def _():
                pltpu.make_async_copy(slots(slot), slots(slot), recv.at[slot]).wait()

            @pl.when(jnp.logical_not(local))
            def _():
                remote(slots(slot), slots(slot), send.at[0], recv.at[slot], sibling).wait_recv()

    def g_block(slot, j, bit):
        tall = g_in.shape[0] // 2
        return g_all.at[slot, pl.ds(bit * tall, tall), half_of(j)]

    def g_copy(j, bit, step):
        tall = g_in.shape[0] // 2
        to = sibling if step == 0 else place(x, (y + step) % 4, z, y_lo)
        return remote(
            g_in.at[pl.ds(bit * tall, tall), half_of(j)], g_block(row, j, bit),
            g_s.at[j, bit, step // 2 + (step > 0)], g_r.at[j, row, bit], to,
        )

    def g_start(j):
        for step, bit in ((1, 0), (3, 1), (1, 1), (3, 0)):
            g_copy(j, bit, step).start()
        for bit in range(2):
            @pl.when(straight)
            def _():
                src = g_in.at[pl.ds(bit * (g_in.shape[0] // 2), g_in.shape[0] // 2), half_of(j)]
                pltpu.make_async_copy(src, g_block(row, j, bit), g_r.at[j, row, bit]).start()

            @pl.when(jnp.logical_not(straight))
            def _():
                g_copy(j, bit, 0).start()

    def g_sent(j):
        for bit in range(2):
            for step in (1, 3):
                g_copy(j, bit, step).wait_send()

            @pl.when(jnp.logical_not(straight))
            def _():
                g_copy(j, bit, 0).wait_send()

    def g_slot(step, which):
        return ((y + step) % 4) // 2 * 2 + which

    def g_pass(j, which, step):
        ref = g_block(g_slot(4 - step, which), j, step // 2)
        return remote(
            ref, ref, f_s.at[j, which, step // 2], g_r.at[j, g_slot(4 - step, which), step // 2],
            place(x, (y + step) % 4, z, core),
        )

    def g_got(slot, j, bit):
        ref = g_block(slot, j, bit)
        remote(ref, ref, g_s.at[j, bit, 0], g_r.at[j, slot, bit], sibling).wait_recv()

    def g_relay(j):
        @pl.when(jnp.logical_not(straight))
        def _():
            for step in (1, 3):
                for which in range(2):
                    g_got(g_slot(4 - step, which), j, step // 2)
                    g_pass(j, which, step).start()

    def g_relayed(j):
        @pl.when(jnp.logical_not(straight))
        def _():
            for step in (1, 3):
                for which in range(2):
                    g_pass(j, which, step).wait_send()

    def arrive_g(j):
        @pl.when(straight)
        def _():
            for bit in range(2):
                own = g_block(row, j, bit)
                pltpu.make_async_copy(own, own, g_r.at[j, row, bit]).wait()
                g_got(g_slot(0, other), j, bit)
                for which in range(2):
                    g_got(g_slot(2, which), j, bit)

        @pl.when(jnp.logical_not(straight))
        def _():
            for step in (1, 3):
                for which in range(2):
                    g_got(g_slot(4 - step, which), j, 1 - step // 2)

    odd = x % 2
    turned = place(x, ((core + odd) % 2) * 2 + y_hi, z, y_lo)
    still = jnp.logical_and(jnp.logical_and(y_hi == y_lo, y_lo == core), odd == 0)

    def b_rows(index):
        return pl.ds(index * (b_in.shape[0] // 2), b_in.shape[0] // 2)

    def turn_start(bit):
        src, dst = b_in.at[b_rows(bit), :], b_all.at[core, x, b_rows(bit), :]

        @pl.when(still)
        def _():
            pltpu.make_async_copy(src, dst, turn_r.at[bit]).start()

        @pl.when(jnp.logical_not(still))
        def _():
            to_slot = b_all.at[y_lo, x, b_rows(bit), :]
            remote(src, to_slot, turn_s.at[bit], turn_r.at[bit], turned).start()

    def turn_wait(bit):
        src, dst = b_in.at[b_rows(bit), :], b_all.at[core, x, b_rows(bit), :]

        @pl.when(still)
        def _():
            pltpu.make_async_copy(src, dst, turn_r.at[bit]).wait()

        @pl.when(jnp.logical_not(still))
        def _():
            arrived = remote(src, dst, turn_s.at[bit], turn_r.at[bit], turned)
            arrived.wait_recv()
            arrived.wait_send()

    def along_x(step, part):
        ref = b_all.at[core, x, b_rows(part), :]
        return remote(ref, ref, bx_s.at[step // 2, part], bx_r.at[step // 2, part], place((x + step) % 4, y, z, core))

    def along_x_wait(step, part):
        ref = b_all.at[core, (x + 4 - step) % 4, b_rows(part), :]
        remote(ref, ref, bx_s.at[step // 2, part], bx_r.at[step // 2, part], sibling).wait_recv()

    def pass_x(step, part):
        ref = b_all.at[core, (x + 4 - step) % 4, b_rows(part), :]
        return remote(ref, ref, bx_s.at[2, part], bx_r.at[2, part], place((x + step) % 4, y, z, core))

    def pass_x_wait(part):
        ref = b_all.at[core, (x + 2) % 4, b_rows(part), :]
        remote(ref, ref, bx_s.at[2, part], bx_r.at[2, part], sibling).wait_recv()

    def across_b(step):
        ref = b_all.at[core, (x + 4 - step) % 4]
        return remote(ref, ref, bc_s.at[step], bc_r.at[step], sibling)

    def across_b_wait(step):
        ref = b_all.at[other, (x + 4 - step) % 4]
        remote(ref, ref, bc_s.at[step], bc_r.at[step], sibling).wait_recv()

    def give(p, j, step):
        block = (span(p), half_of(j))
        if step == 2:
            src, dst, to = far.at[block], far_in.at[block], relay(j)
        else:
            src, dst, to = terms.at[(step // 2 + 1,) + block], terms_in.at[(step // 2,) + block], step
        return remote(src, dst, t_s.at[p, j, step - 1], t_r.at[p, j, step - 1], place((x + to) % 4, y, z, core))

    def relay(j):
        return 1 if j == 0 else 3

    def block_of(owner):
        return (owner % 2) * 2 + (owner // 2 + y_hi) % 2

    def update_to(p, away, step):
        return remote(
            u_out.at[step - 1, away, span(p), :], u_in.at[step - 1, away, span(p), :],
            u_s.at[p, away, step - 1], u_r.at[p, away, step - 1], place(x, y, (z + step) % 4, core),
        )

    def cross(p):
        return remote(
            cross_out.at[span(p), :], cross_in.at[span(p), :], c_s.at[p], c_r.at[p], place(x, (y + 2) % 4, z, core)
        )

    for p in range(LOADS):
        turn_start(p)
        swap_start(p)
    for p in range(LOADS):
        turn_wait(p)
        for step in (1, 3):
            along_x(step, p).start()
        swap_wait(p)
        for step in (2, 1, 3):
            along_z(p, step).start()
        across_a(p, 0).start()
        g_start(p)
    across_b(0).start()

    def first_product(p, j, step):
        owner = (x + step) % 4

        def tile(index, _):
            columns = pl.ds(pl.multiple_of(j * side + index * TILE, TILE), TILE)
            left = jnp.concatenate([a_all[slot, owner, span(p), :] for slot in range(8)], axis=1)
            right = jnp.concatenate([g_all[slot, :, columns] for slot in range(4)], axis=0)
            product = jnp.dot(left, right, preferred_element_type=F32)
            if step == 2:
                far[span(p), columns] = product.astype(BF16)
            elif step == relay(j):
                terms[(step + 1) // 2, span(p), columns] = product + far_in[span(p), columns].astype(F32)
            else:
                terms[(step + 1) // 2, span(p), columns] = product
            return 0

        lax.fori_loop(0, side // TILE, tile, 0)

    def second_product(p, away, step):
        upper = (y_hi + away) % 2
        block = block_of((z + step) % 4)
        left = jnp.concatenate([h_all[upper * 2 + slot, span(p), :] for slot in range(2)], axis=1)
        right = jnp.concatenate([b_all[slot, block] for slot in range(2)], axis=0)
        product = jnp.dot(left, right, preferred_element_type=F32)
        if step == 0:
            u_own[away, span(p), :] = product
        else:
            u_out[step - 1, away, span(p), :] = product.astype(BF16)

    def share_b():
        for step, bit in ((1, 1), (3, 0)):
            along_x_wait(step, bit)
            across_b(step).start()
        for bit in range(2):
            pass_x_wait(bit)
        across_b(2).start()

    def arrive_a(p):
        for step in (1, 3, 2):
            along_z_wait(p, step)
            across_a(p, step).start()
        for step in range(4):
            across_a_wait(p, step)

    def send_far(p, j):
        first_product(p, j, 2)
        give(p, j, 2).start()

    def send_near(p, j):
        for step in (4 - relay(j), relay(j)):
            if step == relay(j):
                give(p, j, 2).wait_recv()
            first_product(p, j, step)
            give(p, j, step).start()
        first_product(p, j, 0)

    def send_terms(chunks):
        send_far(*chunks[0])
        for now, later in zip(chunks, chunks[1:] + [None]):
            if later is not None:
                send_far(*later)
            send_near(*now)

    def sum_terms(p):
        for j in range(SIDES):
            for step in (1, 3):
                give(p, j, step).wait_recv()
        total = terms[0, span(p), :]
        for step in range(2):
            total += terms_in[step, span(p), :]
        own_h[span(p), :] = total.astype(BF16)
        spread_start(own_h.at[span(p), :], h_all.at[row, span(p), :], h_s.at[p], h_r.at[p])

    g_relay(0)
    arrive_a(0)
    for step, bit in ((1, 0), (3, 1)):
        along_x_wait(step, bit)
        pass_x(step, bit).start()
    g_relay(1)
    arrive_g(0)
    early = list(range(PARTS // 2))
    send_terms([(p, 0) for p in early])
    arrive_a(1)
    arrive_g(1)
    def send_update(p):
        spread_wait(lambda slot: h_all.at[slot, span(p), :], h_s.at[p], h_r.at[p])
        for away in (1, 0):
            for step in (2, 1, 3):
                second_product(p, away, step)
                update_to(p, away, step).start()
            second_product(p, away, 0)

    def sum_update(p, away):
        for step in (1, 3, 2):
            update_to(p, away, step).wait_recv()
        total = u_own[away, span(p), :]
        for step in range(3):
            total += u_in[step, away, span(p), :].astype(F32)
        return total

    half = (z // 2 + y_hi) % 2

    def place_update(p):
        cross_out[span(p), :] = sum_update(p, 1).astype(BF16)
        cross(p).start()
        out[span(p), pl.ds(pl.multiple_of(half * quarter, quarter), quarter)] = sum_update(p, 0)

    send_far(0, 1)
    send_far(1, 1)
    send_near(0, 1)
    send_far(2, 0)
    send_near(1, 1)
    share_b()
    send_far(2, 1)
    send_near(2, 0)
    sum_terms(0)
    send_far(3, 0)
    send_near(2, 1)
    sum_terms(1)
    send_far(3, 1)
    send_near(3, 0)
    send_near(3, 1)
    sum_terms(2)
    for step in range(4):
        across_b_wait(step)
    for p in range(PARTS):
        send_update(p)
        if p == 0:
            sum_terms(3)
        if p >= 1:
            place_update(p - 1)
    place_update(PARTS - 1)
    for p in range(PARTS):
        cross(p).wait_recv()
        out[span(p), pl.ds(pl.multiple_of((1 - half) * quarter, quarter), quarter)] = cross_in[span(p), :].astype(F32)

    for j in range(SIDES):
        g_sent(j)
        g_relayed(j)
    for step in (1, 3):
        for bit in range(2):
            along_x(step, bit).wait_send()
        pass_x(step, step // 2).wait_send()
    for step in range(4):
        across_b(step).wait_send()
    for p in range(LOADS):
        for step in (1, 2, 3):
            along_z(p, step).wait_send()
        for step in range(4):
            across_a(p, step).wait_send()
    for p in range(PARTS):
        for j in range(SIDES):
            for step in (1, 2, 3):
                give(p, j, step).wait_send()
        spread_sent(own_h.at[span(p), :], h_all.at[row, span(p), :], h_s.at[p], h_r.at[p])
        for away in range(2):
            for step in (1, 2, 3):
                update_to(p, away, step).wait_send()
        cross(p).wait_send()


def shards(out_factor, gradient, in_factor):
    height, width = gradient.shape
    dma = pltpu.SemaphoreType.DMA
    return pl.pallas_call(
        kernel,
        out_shape=jax.ShapeDtypeStruct((height, width), F32),
        in_specs=[pl.BlockSpec(memory_space=pl.ANY)] * 3,
        out_specs=pl.BlockSpec(memory_space=pltpu.VMEM),
        scratch_shapes=[
            pltpu.VMEM((8, 4, height, out_factor.shape[1]), BF16),
            pltpu.VMEM((4, height, width), BF16),
            pltpu.VMEM((2, 4) + in_factor.shape, BF16),
            pltpu.VMEM((3, height, width), F32),
            pltpu.VMEM((2, height, width), F32),
            pltpu.VMEM((height, width), BF16),
            pltpu.VMEM((height, width), BF16),
            pltpu.VMEM((height, width), BF16),
            pltpu.VMEM((4, height, width), BF16),
            pltpu.VMEM((3, 2, height, in_factor.shape[1]), BF16),
            pltpu.VMEM((2, height, in_factor.shape[1]), F32),
            pltpu.VMEM((3, 2, height, in_factor.shape[1]), BF16),
            pltpu.VMEM((height, in_factor.shape[1]), BF16),
            pltpu.VMEM((height, in_factor.shape[1]), BF16),
            dma((LOADS,)), dma((LOADS,)),
            dma((LOADS, 3)), dma((LOADS, 3)),
            dma((LOADS, 4)), dma((LOADS, 4)),
            dma((SIDES, 2, 3)), dma((SIDES, 4, 2)), dma((SIDES, 2, 2)),
            dma((2,)), dma((2,)),
            dma((3, 2)), dma((3, 2)),
            dma((4,)), dma((4,)),
            dma((PARTS, SIDES, 3)), dma((PARTS, SIDES, 3)),
            dma((PARTS, 4)), dma((PARTS, 4)),
            dma((PARTS, 2, 3)), dma((PARTS, 2, 3)),
            dma((PARTS,)), dma((PARTS,)),
        ],
        compiler_params=pltpu.CompilerParams(
            collective_id=0, has_side_effects=True, vmem_limit_bytes=60 * 2**20
        ),
        cost_estimate=pl.CostEstimate(flops=2 * 2**34, bytes_accessed=8 * 2**20, transcendentals=0),
    )(out_factor.reshape(4, height, -1), gradient, in_factor)


def solution(mesh):
    in_specs = (P("row", ("depth", "col")), P(("depth", "row"), "col"), P("col", ("row", "depth")))
    out_specs = P(("row", "depth"), "col")
    return jax.shard_map(shards, mesh=mesh, in_specs=in_specs, out_specs=out_specs, check_vma=False)
```
